256 devices in a mesh: rep: 8 (over y_lo, x), row: 32 (over z, y_hi, core).
Axes of the slice: x: 4, y: 4 (y_hi: 2, y_lo: 2; y = y_hi * 2 + y_lo), z: 8, core: 2. Of those that a mesh axis runs over, the one named last changes fastest.
Arguments:
- features: bfloat16 [8, 1024, 16384], P('rep', 'row'), may hold values from -6 to 6
- tile_tgt: int32 [8, 32, 8, 4], P('rep', 'row'), may hold values from 0 to 7
- tile_src: int32 [8, 32, 8, 4], P('rep', 'row'), may hold values from 0 to 127
- tile_count: int32 [8, 32, 8], P('rep', 'row'), may hold values from 1 to 4, as said below
- tile_vals: bfloat16 [8, 32, 8, 4, 128, 128], P('rep', 'row'), may hold values from -0.4375 to 0.4375
- weight: bfloat16 [1024, 1024], P('row'), may hold values from -0.1875 to 0.1875
- cotangent: bfloat16 [262144, 1024], P(('rep', 'row')), may hold values from -6 to 6
Outputs:
- activations: bfloat16 [262144, 1024], P(('rep', 'row'))
- weight_grad: float32 [1024, 1024], P('row')
The draws below stay inside these ranges and needn't reach their ends.
Inputs may be any that keep to these rules, and one draw needn't show every extreme that they name: `tile_count`: slots at or past a device's count in a section are ignored. In every section some device has exactly 4 live slots.
All inputs are finite; a program needn't handle non-finite values.
Results may differ from the reference program's by a relative error of at most 0.015.
Values may be sent and summed in bfloat16 or wider, within the bound.
No kernel may reach another device: no remote copies, remote signals or barrier semaphores. Data moves between devices by JAX's collectives and lax.ppermute only.
A program may use at most 128 MiB of HBM per device.

```python
import math
import jax
import jax.numpy as jnp
from jax import lax

D = 1024
F = 1024
BLK = 128
TGT_DEV = 1024
PANEL = 16384
MAXT = 4
SECTIONS = 8
GROUP = 32
TGT = 262144
N_REP = 8
N_ROW = 32


def draw_tile_count(key, part):
    first_key, second_key, third_key = jax.random.split(key, 3)
    num_devices = SECTIONS * GROUP
    first_draw = jax.random.randint(first_key, (num_devices, SECTIONS), 1, MAXT + 1)
    second_draw = jax.random.randint(second_key, (num_devices, SECTIONS), 1, MAXT + 1)
    counts = jnp.minimum(first_draw, second_draw)
    chosen = jax.random.randint(third_key, (SECTIONS,), 0, num_devices)
    device_ids = jnp.arange(num_devices)[:, None]
    counts = jnp.where(device_ids == chosen[None, :], MAXT, counts)
    return counts.reshape(SECTIONS, GROUP, SECTIONS).astype(jnp.int32)


def plant(array, key, low, top_value):
    shape = array.shape
    place = [jax.random.randint(jax.random.fold_in(key, axis), (), 0, shape[axis]) for axis in range(len(shape))]
    array = array.at[tuple(place)].set(low)
    longest = shape.index(max(shape))
    place[longest] = (place[longest] + 1) % shape[longest]
    return array.at[tuple(place)].set(top_value)


def level_of(stream_key, shape, cuts, low, high):
    def one(dim, shards_of):
        draws = jax.random.uniform(jax.random.fold_in(jax.random.fold_in(stream_key, 6), dim), (shards_of,), jnp.float32, low / len(cuts), high / len(cuts))
        return jnp.repeat(jnp.exp(draws), shape[dim] // shards_of).reshape((-1,) + (1,) * (len(shape) - dim - 1))

    level = one(*cuts[0])
    for cut in cuts[1:]:
        level = level * one(*cut)
    return level


def gaussian(stream_key, shape, deviation, bound, cuts=(), kind=jnp.bfloat16):
    entries = deviation * jax.random.normal(stream_key, shape, jnp.float32)
    if cuts:
        entries = entries * level_of(stream_key, shape, cuts, -0.22, 0.18)
    return jnp.clip(entries, -bound, bound).astype(kind)


def setup_inputs(seed: int = 0) -> dict:
    splits = jax.random.split(jax.random.key(seed), 8)
    return {
        "features": gaussian(splits[0], (SECTIONS, D, PANEL), 1.0, 6.0, ((0, 8), (1, 32))),
        "tile_tgt": plant(jax.random.randint(splits[1], (N_REP, N_ROW, SECTIONS, MAXT), 0, TGT_DEV // BLK), jax.random.fold_in(splits[1], 1), 0, (TGT_DEV // BLK) - 1).astype(jnp.int32),
        "tile_src": plant(jax.random.randint(splits[2], (N_REP, N_ROW, SECTIONS, MAXT), 0, PANEL // BLK), jax.random.fold_in(splits[2], 1), 0, (PANEL // BLK) - 1).astype(jnp.int32),
        "tile_count": draw_tile_count(jax.random.fold_in(splits[7], 71), 0),
        "tile_vals": gaussian(splits[4], (N_REP, N_ROW, SECTIONS, MAXT, BLK, BLK), (BLK * N_REP * MAXT * BLK // (3 * TGT_DEV)) ** -0.5, 0.4375, ((0, 8), (1, 32))),
        "weight": gaussian(splits[5], (D, F), D ** -0.5, 0.1875, ((0, 32),)),
        "cotangent": gaussian(splits[6], (TGT, F), 1.0, 6.0, ((0, 256),)),
    }


def silu_grad(preact):
    sigmoid_val = jax.nn.sigmoid(preact)
    return sigmoid_val * (1.0 + preact * (1.0 - sigmoid_val))

def reference(features, tile_tgt, tile_src, tile_count, tile_vals, weight, cotangent):
    num_devices = N_REP * N_ROW
    num_blocks = TGT_DEV // BLK
    panels = features.reshape(SECTIONS, D, PANEL // BLK, BLK)
    targets = tile_tgt.reshape(num_devices, SECTIONS, MAXT)
    sources = tile_src.reshape(num_devices, SECTIONS, MAXT)
    counts = tile_count.reshape(num_devices, SECTIONS)
    values = tile_vals.reshape(num_devices, SECTIONS, MAXT, BLK, BLK)
    cot_rows = cotangent.reshape(num_devices, TGT_DEV, F)
    section_ids = jnp.arange(SECTIONS, dtype=jnp.int32)[:, None]
    block_ids = jnp.arange(num_blocks, dtype=jnp.int32)[:, None, None]
    slot_ids = jnp.arange(MAXT, dtype=jnp.int32)[None, None, :]

    def one_device(grad_total, inputs):
        tgt_dev, src_dev, count_dev, value_dev, cot_dev = inputs
        blocks = panels[section_ids, :, src_dev]
        contrib = jnp.einsum('smij,smdj->smid', value_dev.astype(jnp.float32), blocks.astype(jnp.float32))
        select = ((tgt_dev[None] == block_ids) & (slot_ids < count_dev[None, :, None])).astype(jnp.float32)
        aggregate = jnp.einsum('bsm,smid->bid', select, contrib)
        mixed = aggregate.reshape(TGT_DEV, D).astype(jnp.bfloat16)
        preact = jnp.dot(mixed, weight, preferred_element_type=jnp.float32)
        output = jax.nn.silu(preact).astype(jnp.bfloat16)
        dpre = (cot_dev.astype(jnp.float32) * silu_grad(preact)).astype(jnp.bfloat16)
        term = lax.dot_general(mixed, dpre, (((0,), (0,)), ((), ())), preferred_element_type=jnp.float32)
        return (grad_total + term, output)
    grad_total, outputs = lax.scan(one_device, jnp.zeros((D, F), jnp.float32), (targets, sources, counts, values, cot_rows))
    return (outputs.reshape(TGT, F), grad_total / math.sqrt(TGT))
```

```python
import functools
import math

import jax
import jax.numpy as jnp
from jax import lax
from jax.experimental import pallas as pl
from jax.experimental.pallas import tpu as pltpu
from jax.sharding import Mesh, PartitionSpec as P

REP = ("ylo", "x")
PLANE = ("ylo", "x", "yhi", "core")
CHIPS_XY = ("ylo", "x", "yhi")
ZN = 8
PARTS = ((0, 1, -1), (2, -2), (3, -3, 4))
VMEM = pl.BlockSpec(memory_space=pltpu.VMEM)
SMEM = pl.BlockSpec(memory_space=pltpu.SMEM)


def silu_grad(preact):
    sigmoid_val = jax.nn.sigmoid(preact)
    return sigmoid_val * (1.0 + preact * (1.0 - sigmoid_val))


def shift_z(value, step):
    return lax.ppermute(value, "z", [(i, (i + step) % ZN) for i in range(ZN)])


def exchange(value, axes):
    return lax.all_to_all(value, axes, split_axis=0, concat_axis=0, tiled=True)


def pick_kernel(pieces, block, wanted_ref, *refs):
    slices, out_ref = refs[:-1], refs[-1]
    slots = out_ref.shape[1]

    def one(step, carry):
        dest, slot = step // slots, step % slots
        start = pl.multiple_of(wanted_ref[dest, slot] * block, block)
        for ref, (place, low, high) in zip(slices, pieces):
            out_ref[dest, slot, place, low:high, :] = ref[:, pl.ds(start, block)]
        return carry

    lax.fori_loop(0, out_ref.shape[0] * slots, one, 0, unroll=4)


def pick(wanted, slices, pieces, places, rows, block):
    askers, slots = wanted.shape
    return pl.pallas_call(
        functools.partial(pick_kernel, pieces, block),
        out_shape=jax.ShapeDtypeStruct((askers, slots, places, rows, block), jnp.bfloat16),
        in_specs=[SMEM] + [VMEM] * len(slices),
        out_specs=VMEM,
        compiler_params=pltpu.CompilerParams(vmem_limit_bytes=40 * 2**20),
        cost_estimate=pl.CostEstimate(flops=0, bytes_accessed=len(slices) * 2**21, transcendentals=0),
    )(wanted, *slices)


def aggregate_kernel(zs_of, z_ref, tgt_ref, count_ref, vals_ref, *refs):
    parts, out_ref, acc = refs[: len(zs_of)], refs[-2], refs[-1]
    sections, slots, block, _ = vals_ref.shape
    rows = parts[0].shape[3]
    lanes = parts[0].shape[0] // sections
    acc[...] = jnp.zeros_like(acc)

    def one(step, carry):
        section, slot = step // slots, step % slots

        @pl.when(slot < count_ref[section])
        def _():
            column = pl.multiple_of(tgt_ref[section, slot] * block, block)
            tile = vals_ref[section, slot]
            for part, places in zip(parts, zs_of):
                for lane in range(lanes):
                    columns_in = part[section * lanes + lane, slot].reshape(len(places) * rows, block)
                    contrib = lax.dot_general(
                        columns_in, tile, (((1,), (1,)), ((), ())), preferred_element_type=jnp.float32
                    )
                    for index, place in enumerate(places):
                        low = pl.multiple_of((z_ref[place] * lanes + lane) * rows, rows)
                        acc[pl.ds(low, rows), pl.ds(column, block)] += contrib[index * rows : (index + 1) * rows]

        return carry

    lax.fori_loop(0, sections * slots, one, 0)
    out_ref[...] = acc[...].astype(out_ref.dtype)


def aggregate(zs, targets, counts, values, parts, zs_of, num_rows, num_feats):
    return pl.pallas_call(
        functools.partial(aggregate_kernel, zs_of),
        out_shape=jax.ShapeDtypeStruct((num_feats, num_rows), jnp.bfloat16),
        in_specs=[SMEM] * 3 + [VMEM] * (1 + len(parts)),
        out_specs=VMEM,
        scratch_shapes=[pltpu.VMEM((num_feats, num_rows), jnp.float32)],
        compiler_params=pltpu.CompilerParams(vmem_limit_bytes=48 * 2**20),
        cost_estimate=pl.CostEstimate(flops=10**9, bytes_accessed=12 * 2**20, transcendentals=0),
    )(zs, targets, counts, values, *parts)


def sum_over_devices(partial):
    rows, cols = partial.shape
    core, other = lax.axis_index("core"), 1 - lax.axis_index("core")
    halves = partial.reshape(16, 2, rows // 32, cols)
    gone = lax.dynamic_index_in_dim(halves, other, 1, keepdims=False).astype(jnp.bfloat16)
    kept = lax.dynamic_index_in_dim(halves, core, 1, keepdims=False)
    came = lax.ppermute(gone, "core", [(0, 1), (1, 0)])
    chip = (kept + came.astype(jnp.float32)).astype(jnp.bfloat16)
    chip = chip.reshape(8, 2, rows // 32, 8, cols // 8).transpose(3, 1, 0, 2, 4)
    chip = chip.reshape(16, 8, rows // 32, cols // 8)
    plane = exchange(chip, CHIPS_XY).astype(jnp.float32).sum(0)
    column = exchange(plane, "z").sum(0)
    whole = exchange(jnp.broadcast_to(column[None], (8, *column.shape)), REP)
    return whole.transpose(1, 0, 2).reshape(rows // 32, cols)


def per_device(features, tile_tgt, tile_src, tile_count, tile_vals, weight, cotangent):
    group_size = 32
    block_size = tile_vals.shape[-1]
    rows = features.shape[1]
    feat_width = rows * group_size
    tgt_rows = cotangent.shape[0]
    targets, sources, counts, values = tile_tgt[0, 0], tile_src[0, 0], tile_count[0, 0], tile_vals[0, 0]

    whole_weight = lax.all_gather(weight, ("z", "yhi", "core"), axis=0, tiled=True)
    wanted = exchange(jnp.repeat(sources, 4, axis=0)[:, None, :], PLANE)[:, 0]

    held = {0: features[0]}
    for step in range(1, 4):
        held[step] = shift_z(held[step - 1], 1)
        held[-step] = shift_z(held[1 - step], -1)
    up, down = shift_z(held[3][: rows // 2], 1), shift_z(held[-3][rows // 2 :], -1)

    arrived = []
    for distances in PARTS:
        slices, pieces = [], []
        for place, distance in enumerate(distances):
            if distance == 4:
                slices += [up, down]
                pieces += [(place, 0, rows // 2), (place, rows // 2, rows)]
            else:
                slices.append(held[distance])
                pieces.append((place, 0, rows))
        picked = pick(wanted, slices, tuple(pieces), len(distances), rows, block_size)
        arrived.append(exchange(picked, PLANE))
    order = [d for distances in PARTS for d in distances]
    zs = lax.rem(lax.axis_index("z") + ZN - jnp.array(order, jnp.int32), ZN)
    places = iter(range(len(order)))
    zs_of = tuple(tuple(next(places) for _ in distances) for distances in PARTS)
    mixed_t = aggregate(zs, targets, counts, values, arrived, zs_of, tgt_rows, feat_width)

    preact = lax.dot_general(
        mixed_t, whole_weight, (((0,), (0,)), ((), ())), preferred_element_type=jnp.float32
    )
    activations = jax.nn.silu(preact).astype(jnp.bfloat16)
    dpre = (cotangent.astype(jnp.float32) * silu_grad(preact)).astype(jnp.bfloat16)
    partial = jnp.dot(mixed_t, dpre, preferred_element_type=jnp.float32)
    total_rows = tgt_rows * 8 * group_size
    weight_grad = sum_over_devices(partial) / math.sqrt(total_rows)
    return (activations, weight_grad)


def solution(mesh):
    row = ("z", "yhi", "core")
    fine = Mesh(mesh.devices.reshape(2, 4, 8, 2, 2), ("ylo", "x", "z", "yhi", "core"))
    in_specs = (
        P(REP, row, None),
        P(REP, row, None, None),
        P(REP, row, None, None),
        P(REP, row, None),
        P(REP, row, None, None, None, None),
        P(row, None),
        P(REP + row, None),
    )
    out_specs = (P(REP + row, None), P(row, None))
    return jax.shard_map(per_device, mesh=fine, in_specs=in_specs, out_specs=out_specs, check_vma=False)
```

```python
import functools
import math

import jax
import jax.numpy as jnp
from jax import lax
from jax.experimental import pallas as pl
from jax.experimental.pallas import tpu as pltpu
from jax.sharding import Mesh, PartitionSpec as P

REP = ("ylo", "x")
PLANE = ("ylo", "x", "yhi", "core")
CHIPS_XY = ("ylo", "x", "yhi")
ZN = 8
PARTS = ((0, 1, -1), (2, -2), (3, -3, 4))
PICK_COSTS = (20, 20, 20)
ORDER = tuple(d for part in PARTS for d in part)
VMEM = pl.BlockSpec(memory_space=pltpu.VMEM)
SMEM = pl.BlockSpec(memory_space=pltpu.SMEM)


def silu_grad(preact):
    sigmoid_val = jax.nn.sigmoid(preact)
    return sigmoid_val * (1.0 + preact * (1.0 - sigmoid_val))


def shift_z(value, step):
    return lax.ppermute(value, "z", [(i, (i + step) % ZN) for i in range(ZN)])


def exchange(value, axes):
    return lax.all_to_all(value, axes, split_axis=0, concat_axis=0, tiled=True)


def pick_kernel(pieces, block, wanted_ref, *refs):
    slices, out_ref = refs[:-1], refs[-1]
    slots = out_ref.shape[1]

    def one(step, carry):
        dest, slot = step // slots, step % slots
        start = pl.multiple_of(wanted_ref[dest, slot] * block, block)
        for ref, (place, low, high) in zip(slices, pieces):
            out_ref[dest, slot, place, low:high, :] = ref[:, pl.ds(start, block)]
        return carry

    lax.fori_loop(0, out_ref.shape[0] * slots, one, 0, unroll=4)


def pick(wanted, slices, pieces, places, rows, block, cost):
    askers, slots = wanted.shape
    return pl.pallas_call(
        functools.partial(pick_kernel, pieces, block),
        out_shape=jax.ShapeDtypeStruct((askers, slots, places, rows, block), jnp.bfloat16),
        in_specs=[SMEM] + [VMEM] * len(slices),
        out_specs=VMEM,
        compiler_params=pltpu.CompilerParams(vmem_limit_bytes=40 * 2**20),
        cost_estimate=pl.CostEstimate(flops=cost * 10**9, bytes_accessed=len(slices) * 2**21, transcendentals=0),
    )(wanted, *slices)


def aggregate_kernel(core_ref, tgt_ref, count_ref, vals_ref, part, out_ref, acc):
    sections, slots, block, _ = vals_ref.shape
    places, rows = part.shape[2:4]
    lanes = part.shape[0] // sections
    acc[...] = jnp.zeros_like(acc)
    core = core_ref[0]

    def one(step, carry):
        section, slot = step // slots, step % slots

        @pl.when(slot < count_ref[section])
        def _():
            column = pl.multiple_of(tgt_ref[section, slot] * block, block)
            tile = vals_ref[section, slot]
            for lane in range(lanes):
                source = section * lanes + lane + core * (1 - 2 * (lane % 2))
                columns_in = part[source, slot].reshape(places * rows, block)
                contrib = lax.dot_general(
                    columns_in, tile, (((1,), (1,)), ((), ())), preferred_element_type=jnp.float32
                )
                for place in range(places):
                    low = (place * lanes + lane) * rows
                    acc[low : low + rows, pl.ds(column, block)] += contrib[place * rows : (place + 1) * rows]

        return carry

    lax.fori_loop(0, sections * slots, one, 0)
    out_ref[...] = acc[...].astype(out_ref.dtype)


def aggregate(core, targets, counts, values, part, num_rows):
    sections = values.shape[0]
    num_feats = part.shape[0] // sections * part.shape[2] * part.shape[3]
    return pl.pallas_call(
        aggregate_kernel,
        out_shape=jax.ShapeDtypeStruct((num_feats, num_rows), jnp.bfloat16),
        in_specs=[SMEM] * 3 + [VMEM] * 2,
        out_specs=VMEM,
        scratch_shapes=[pltpu.VMEM((num_feats, num_rows), jnp.float32)],
        compiler_params=pltpu.CompilerParams(vmem_limit_bytes=32 * 2**20),
        cost_estimate=pl.CostEstimate(flops=3 * 10**9, bytes_accessed=8 * 2**20, transcendentals=0),
    )(core, targets, counts, values, part)


def sum_plane_kernel(z_ref, came_ref, out_ref):
    for place, distance in enumerate(ORDER):
        total = came_ref[:, place].astype(jnp.float32).sum(0)
        out_ref[lax.rem(z_ref[0] + (ZN - distance), ZN)] = total


def sum_plane(came):
    return pl.pallas_call(
        sum_plane_kernel,
        out_shape=jax.ShapeDtypeStruct(came.shape[1:], jnp.float32),
        in_specs=[SMEM, VMEM],
        out_specs=VMEM,
        compiler_params=pltpu.CompilerParams(vmem_limit_bytes=16 * 2**20),
    )(lax.axis_index("z").astype(jnp.int32)[None], came)


def sum_over_devices(partial):
    zs, _, _, rows, cols = partial.shape
    came = lax.ppermute(partial[:, :, 1].astype(jnp.bfloat16), "core", [(0, 1), (1, 0)])
    chip = (partial[:, :, 0] + came.astype(jnp.float32)).astype(jnp.bfloat16)
    chip = chip.reshape(zs, 2, rows, 8, cols // 8).transpose(3, 1, 0, 2, 4)
    chip = chip.reshape(16, zs, rows, cols // 8)
    plane = sum_plane(exchange(chip, CHIPS_XY))
    column = exchange(plane, "z").sum(0)
    whole = exchange(jnp.broadcast_to(column[None], (8, *column.shape)), REP)
    return whole.transpose(1, 0, 2).reshape(rows, cols)


def whole_weight(own):
    flip = [(0, 3), (1, 2), (2, 1), (3, 0)]
    other = lax.ppermute(own, ("ylo", "yhi"), flip)
    first = lax.axis_index("yhi") == 0
    both = jnp.stack([jnp.where(first, own, other), jnp.where(first, other, own)], axis=1)
    return jnp.stack([both, lax.ppermute(both, "core", [(0, 1), (1, 0)])], axis=2)


def per_device(features, tile_tgt, tile_src, tile_count, tile_vals, weight, cotangent):
    group_size = 32
    block_size = tile_vals.shape[-1]
    rows, panel = features.shape[1:]
    tgt_rows, out_width = cotangent.shape
    targets, sources, counts, values = tile_tgt[0, 0], tile_src[0, 0], tile_count[0, 0], tile_vals[0, 0]

    wanted = exchange(jnp.repeat(sources, 4, axis=0)[:, None, :], PLANE)[:, 0]

    held = {0: jnp.concatenate([features[0], weight], axis=1)}
    for step in range(1, 4):
        held[step] = shift_z(held[step - 1], 1)
        held[-step] = shift_z(held[1 - step], -1)
    up, down = shift_z(held[3][: rows // 2], 1), shift_z(held[-3][rows // 2 :], -1)

    core = lax.axis_index("core").astype(jnp.int32)[None]
    mixed_t, weights = [], []
    for distances, cost in zip(PARTS, PICK_COSTS):
        slices, pieces = [], []
        for place, distance in enumerate(distances):
            if distance == 4:
                slices += [up, down]
                pieces += [(place, 0, rows // 2), (place, rows // 2, rows)]
                weights.append(jnp.concatenate([up[:, panel:], down[:, panel:]], axis=0))
            else:
                slices.append(held[distance])
                pieces.append((place, 0, rows))
                weights.append(held[distance][:, panel:])
        picked = pick(wanted, slices, tuple(pieces), len(distances), rows, block_size, cost)
        arrived = exchange(picked, PLANE)
        mixed_t.append(aggregate(core, targets, counts, values, arrived, tgt_rows))
    mixed_t = jnp.concatenate(mixed_t, axis=0)
    weight_in = whole_weight(jnp.stack(weights)).reshape(-1, out_width)

    preact = lax.dot_general(mixed_t, weight_in, (((0,), (0,)), ((), ())), preferred_element_type=jnp.float32)
    activations = jax.nn.silu(preact).astype(jnp.bfloat16)
    dpre = (cotangent.astype(jnp.float32) * silu_grad(preact)).astype(jnp.bfloat16)
    partial = jnp.dot(mixed_t, dpre, preferred_element_type=jnp.float32)
    total_rows = tgt_rows * 8 * group_size
    weight_grad = sum_over_devices(partial.reshape(ZN, 2, 2, rows, out_width)) / math.sqrt(total_rows)
    return (activations, weight_grad)


def solution(mesh):
    row = ("z", "yhi", "core")
    fine = Mesh(mesh.devices.reshape(2, 4, 8, 2, 2), ("ylo", "x", "z", "yhi", "core"))
    in_specs = (
        P(REP, row, None),
        P(REP, row, None, None),
        P(REP, row, None, None),
        P(REP, row, None),
        P(REP, row, None, None, None, None),
        P(row, None),
        P(REP + row, None),
    )
    out_specs = (P(REP + row, None), P(row, None))
    return jax.shard_map(per_device, mesh=fine, in_specs=in_specs, out_specs=out_specs, check_vma=False)
```

```python
import functools
import math

import jax
import jax.numpy as jnp
from jax import lax
from jax.experimental import pallas as pl
from jax.experimental.pallas import tpu as pltpu
from jax.sharding import Mesh, PartitionSpec as P

REP = ("ylo", "x")
PLANE = ("ylo", "x", "yhi", "core")
CHIPS_XY = ("ylo", "x", "yhi")
ZN = 8
FIRST = (0, 1, -1)
SECOND = (2, -2, 3, -3, 4)
ORDER = FIRST + SECOND
LANES = 4
VMEM = pl.BlockSpec(memory_space=pltpu.VMEM)
SMEM = pl.BlockSpec(memory_space=pltpu.SMEM)
ANY = pl.BlockSpec(memory_space=pl.ANY)
SWAP = [(0, 1), (1, 0)]


def params(mib):
    return pltpu.CompilerParams(vmem_limit_bytes=mib * 2**20)


def cost(flops, size):
    return pl.CostEstimate(flops=flops, bytes_accessed=size, transcendentals=0)


def shift_z(value, step):
    return lax.ppermute(value, "z", [(i, (i + step) % ZN) for i in range(ZN)])


def exchange(value, axes):
    return lax.all_to_all(value, axes, split_axis=0, concat_axis=0, tiled=True)


def ring(own):
    half = own.shape[0] // 2
    held = {0: own}
    for step in range(1, ZN // 2):
        held[step] = shift_z(held[step - 1], 1)
        held[-step] = shift_z(held[1 - step], -1)
    far = ZN // 2 - 1
    held[ZN // 2] = shift_z(held[far][:half], 1), shift_z(held[-far][half:], -1)
    return held


def pick_into(wanted_ref, slices, places, target, block):
    slots = target.shape[1]

    def one(step, carry):
        dest, slot = step // slots, step % slots
        start = pl.multiple_of(wanted_ref[dest, slot] * block, block)
        for ref, (place, low, high) in zip(slices, places):
            target[dest, slot, place, low:high, :] = ref[:, pl.ds(start, block)]
        return carry

    lax.fori_loop(0, target.shape[0] * slots, one, 0, unroll=4)


def pick_kernel(block, wanted_ref, *refs):
    slices, out_ref = refs[:-1], refs[-1]
    places = [(place, 0, ref.shape[0]) for place, ref in enumerate(slices)]
    pick_into(wanted_ref, slices, places, out_ref, block)


def pick(wanted, slices, block, flops):
    askers, slots = wanted.shape
    return pl.pallas_call(
        functools.partial(pick_kernel, block),
        out_shape=jax.ShapeDtypeStruct((askers, slots, len(slices), slices[0].shape[0], block), jnp.bfloat16),
        in_specs=[SMEM] + [VMEM] * len(slices),
        out_specs=VMEM,
        compiler_params=params(40),
        cost_estimate=cost(flops, len(slices) * 2**21),
    )(wanted, *slices)


def pick_most_kernel(block, wanted_ref, *refs):
    slices, (out_ref, buffer, sem) = refs[:-3], refs[-3:]
    places = [(place, 0, ref.shape[0]) for place, ref in enumerate(slices)]
    pick_into(wanted_ref, slices, places, buffer, block)
    copy = pltpu.make_async_copy(buffer, out_ref.at[:, :, : len(slices)], sem)
    copy.start()
    copy.wait()


def pick_most(wanted, slices, places, block, flops):
    askers, slots = wanted.shape
    rows = slices[0].shape[0]
    return pl.pallas_call(
        functools.partial(pick_most_kernel, block),
        out_shape=jax.ShapeDtypeStruct((askers, slots, places, rows, block), jnp.bfloat16),
        in_specs=[SMEM] + [VMEM] * len(slices),
        out_specs=ANY,
        scratch_shapes=[pltpu.VMEM((askers, slots, len(slices), rows, block), jnp.bfloat16), pltpu.SemaphoreType.DMA],
        compiler_params=params(40),
        cost_estimate=cost(flops, len(slices) * 2**21),
    )(wanted, *slices)


def pick_last_kernel(block, wanted_ref, up_ref, down_ref, _, out_ref, buffer, sem):
    half, rows = up_ref.shape[0], buffer.shape[3]
    pick_into(wanted_ref, (up_ref, down_ref), ((0, 0, half), (0, half, rows)), buffer, block)
    copy = pltpu.make_async_copy(buffer, out_ref.at[:, :, out_ref.shape[2] - 1 :], sem)
    copy.start()
    copy.wait()


def pick_last(wanted, up, down, most, block, flops):
    askers, slots, _, rows, _ = most.shape
    return pl.pallas_call(
        functools.partial(pick_last_kernel, block),
        out_shape=jax.ShapeDtypeStruct(most.shape, most.dtype),
        in_specs=[SMEM, VMEM, VMEM, ANY],
        out_specs=ANY,
        input_output_aliases={3: 0},
        scratch_shapes=[pltpu.VMEM((askers, slots, 1, rows, block), jnp.bfloat16), pltpu.SemaphoreType.DMA],
        compiler_params=params(24),
        cost_estimate=cost(flops, 2**21),
    )(wanted, up, down, most)


def add_tiles(core, tgt_ref, count_ref, vals_ref, part, acc):
    sections, slots, block, _ = vals_ref.shape
    places, rows = part.shape[2:4]
    acc[...] = jnp.zeros_like(acc)

    def one(step, carry):
        section, slot = step // slots, step % slots

        @pl.when(slot < count_ref[section])
        def _():
            column = pl.multiple_of(tgt_ref[section, slot] * block, block)
            sources = [section * LANES + lane + core * (1 - 2 * (lane % 2)) for lane in range(LANES)]
            columns_in = jnp.concatenate([part[source, slot].reshape(places * rows, block) for source in sources])
            contrib = lax.dot_general(
                columns_in, vals_ref[section, slot], (((1,), (1,)), ((), ())), preferred_element_type=jnp.float32
            )
            for lane in range(LANES):
                for place in range(places):
                    low, at = (place * LANES + lane) * rows, (lane * places + place) * rows
                    acc[low : low + rows, pl.ds(column, block)] += contrib[at : at + rows]

        return carry

    lax.fori_loop(0, sections * slots, one, 0)


def aggregate_kernel(core_ref, tgt_ref, count_ref, vals_ref, part, out_ref, acc):
    add_tiles(core_ref[0], tgt_ref, count_ref, vals_ref, part, acc)
    out_ref[...] = acc[...].astype(out_ref.dtype)


def aggregate(core, targets, counts, values, part, num_rows):
    num_feats = LANES * part.shape[2] * part.shape[3]
    return pl.pallas_call(
        aggregate_kernel,
        out_shape=jax.ShapeDtypeStruct((num_feats, num_rows), jnp.bfloat16),
        in_specs=[SMEM] * 3 + [VMEM] * 2,
        out_specs=VMEM,
        scratch_shapes=[pltpu.VMEM((num_feats, num_rows), jnp.float32)],
        compiler_params=params(32),
        cost_estimate=cost(3 * 10**9, 8 * 2**20),
    )(core, targets, counts, values, part)


def layer_kernel(
    core_ref, tgt_ref, count_ref, vals_ref, part, early_ref, weight_ref, cot_ref, act_ref, kept_ref, gone_ref, acc, mixed, dpre
):
    early = early_ref.shape[0]
    add_tiles(core_ref[0], tgt_ref, count_ref, vals_ref, part, acc)
    mixed[:early] = early_ref[...]
    mixed[early:] = acc[...].astype(mixed.dtype)
    step = 256
    for low in range(0, act_ref.shape[0], step):
        at = slice(low, low + step)
        preact = lax.dot_general(
            mixed[:, at], weight_ref[...], (((0,), (0,)), ((), ())), preferred_element_type=jnp.float32
        )
        sigmoid_val = jax.nn.sigmoid(preact)
        act_ref[at] = (preact * sigmoid_val).astype(act_ref.dtype)
        slope = sigmoid_val * (1.0 + preact * (1.0 - sigmoid_val))
        dpre[at] = (cot_ref[at].astype(jnp.float32) * slope).astype(dpre.dtype)
    pieces, his, zs, rows, width = kept_ref.shape
    for low in range(0, mixed.shape[0], step):
        grad = jnp.dot(mixed[low : low + step], dpre[...], preferred_element_type=jnp.float32)
        for at in range(0, step, rows):
            lane = (low + at) // rows
            place, hi, core = lane // LANES, lane % LANES // 2, lane % 2
            for piece in range(pieces):
                value = grad[at : at + rows, piece * width : (piece + 1) * width]
                if core == 0:
                    kept_ref[piece, hi, place] = value
                else:
                    gone_ref[piece, hi, place] = value.astype(gone_ref.dtype)


def layer(core, targets, counts, values, part, early, weight, cotangent):
    tgt_rows, width = cotangent.shape
    feats = weight.shape[0]
    cut = (8, 2, ZN, part.shape[3], width // 8)
    late = feats - early.shape[0]
    return pl.pallas_call(
        layer_kernel,
        out_shape=(
            jax.ShapeDtypeStruct((tgt_rows, width), jnp.bfloat16),
            jax.ShapeDtypeStruct(cut, jnp.float32),
            jax.ShapeDtypeStruct(cut, jnp.bfloat16),
        ),
        in_specs=[SMEM] * 3 + [VMEM] * 5,
        out_specs=(VMEM, VMEM, VMEM),
        scratch_shapes=[
            pltpu.VMEM((late, tgt_rows), jnp.float32),
            pltpu.VMEM((feats, tgt_rows), jnp.bfloat16),
            pltpu.VMEM((tgt_rows, width), jnp.bfloat16),
        ],
        compiler_params=params(48),
        cost_estimate=cost(6 * 10**9, 20 * 2**20),
    )(core, targets, counts, values, part, early, weight, cotangent)


def sum_plane_kernel(z_ref, came_ref, out_ref):
    for place, distance in enumerate(ORDER):
        total = came_ref[:, place].astype(jnp.float32).sum(0)
        out_ref[lax.rem(z_ref[0] + (ZN - distance), ZN)] = total


def sum_plane(came):
    return pl.pallas_call(
        sum_plane_kernel,
        out_shape=jax.ShapeDtypeStruct(came.shape[1:], jnp.float32),
        in_specs=[SMEM, VMEM],
        out_specs=VMEM,
        compiler_params=params(16),
    )(lax.axis_index("z").astype(jnp.int32)[None], came)


def sum_over_devices(kept, gone):
    came = lax.ppermute(gone, "core", SWAP)
    chip = (kept + came.astype(jnp.float32)).astype(jnp.bfloat16)
    chip = chip.reshape(16, *chip.shape[2:])
    plane = sum_plane(exchange(chip, CHIPS_XY))
    column = exchange(plane, "z").sum(0)
    whole = exchange(jnp.broadcast_to(column[None], (8, *column.shape)), REP)
    return whole.transpose(1, 0, 2).reshape(column.shape[0], -1)


def weight_lanes(own):
    other = lax.ppermute(own, ("ylo", "yhi"), [(0, 3), (1, 2), (2, 1), (3, 0)])
    first = lax.axis_index("yhi") == 0
    both = jnp.stack([jnp.where(first, own, other), jnp.where(first, other, own)])
    lanes = jnp.stack([both, lax.ppermute(both, "core", SWAP)], axis=1)
    return lanes.reshape(-1, own.shape[1])


def whole_weight(lanes):
    held = ring(lanes)
    held[ZN // 2] = jnp.concatenate(held[ZN // 2])
    return jnp.concatenate([held[distance] for distance in ORDER])


def per_device(features, tile_tgt, tile_src, tile_count, tile_vals, weight, cotangent):
    block_size = tile_vals.shape[-1]
    tgt_rows = cotangent.shape[0]
    targets, sources, counts, values = tile_tgt[0, 0], tile_src[0, 0], tile_count[0, 0], tile_vals[0, 0]
    core = lax.axis_index("core").astype(jnp.int32)[None]

    wanted = exchange(jnp.repeat(sources, LANES, axis=0)[:, None, :], PLANE)[:, 0]
    wanted, lanes = lax.optimization_barrier((wanted, weight_lanes(weight)))
    held = ring(features[0])
    first = pick(wanted, [held[distance] for distance in FIRST], block_size, PICK_FLOPS[0])
    early = aggregate(core, targets, counts, values, exchange(first, PLANE), tgt_rows)
    most = pick_most(wanted, [held[d] for d in SECOND[:-1]], len(SECOND), block_size, PICK_FLOPS[1])
    second = pick_last(wanted, *held[SECOND[-1]], most, block_size, PICK_FLOPS[2])
    part = exchange(second, PLANE)
    weight_in = whole_weight(lanes)
    activations, kept, gone = layer(core, targets, counts, values, part, early, weight_in, cotangent)
    weight_grad = sum_over_devices(kept, gone) / math.sqrt(tgt_rows * 256)
    return (activations, weight_grad)


PICK_FLOPS = (20 * 10**9, 20 * 10**9, 10**9)


def solution(mesh):
    row = ("z", "yhi", "core")
    fine = Mesh(mesh.devices.reshape(2, 4, 8, 2, 2), ("ylo", "x", "z", "yhi", "core"))
    in_specs = (
        P(REP, row, None),
        P(REP, row, None, None),
        P(REP, row, None, None),
        P(REP, row, None),
        P(REP, row, None, None, None, None),
        P(row, None),
        P(REP + row, None),
    )
    out_specs = (P(REP + row, None), P(row, None))
    return jax.shard_map(per_device, mesh=fine, in_specs=in_specs, out_specs=out_specs, check_vma=False)
```

```python
import functools
import math

import jax
import jax.numpy as jnp
from jax import lax
from jax.experimental import pallas as pl
from jax.experimental.pallas import tpu as pltpu
from jax.sharding import Mesh, PartitionSpec as P

REP = ("ylo", "x")
PLANE = ("ylo", "x", "yhi", "core")
CHIPS_XY = ("ylo", "x", "yhi")
ZN = 8
FIRST = (0, 1, -1)
SECOND = (2, -2, 3, -3, 4)
ORDER = FIRST + SECOND
LANES = 4
VMEM = pl.BlockSpec(memory_space=pltpu.VMEM)
SMEM = pl.BlockSpec(memory_space=pltpu.SMEM)
HBM = pl.BlockSpec(memory_space=pltpu.HBM)
SWAP = [(0, 1), (1, 0)]


def params(mib):
    return pltpu.CompilerParams(vmem_limit_bytes=mib * 2**20)


def cost(flops, size):
    return pl.CostEstimate(flops=flops, bytes_accessed=size, transcendentals=0)


def shift_z(value, step):
    return lax.ppermute(value, "z", [(i, (i + step) % ZN) for i in range(ZN)])


def exchange(value, axes):
    return lax.all_to_all(value, axes, split_axis=0, concat_axis=0, tiled=True)


def ring(upper, lower):
    held = {0: (upper, lower)}
    for step in range(1, ZN // 2):
        for sign in (1, -1):
            before = held[sign * (step - 1)]
            held[sign * step] = shift_z(before[0], sign), shift_z(before[1], sign)
    far = ZN // 2 - 1
    held[ZN // 2] = shift_z(held[far][0], 1), shift_z(held[-far][1], -1)
    return held


def short_ring(own):
    half = own.shape[0] // 2
    held = {0: own}
    for step in range(1, ZN // 2):
        held[step] = shift_z(held[step - 1], 1)
        held[-step] = shift_z(held[1 - step], -1)
    far = ZN // 2 - 1
    held[ZN // 2] = jnp.concatenate([shift_z(held[far][:half], 1), shift_z(held[-far][half:], -1)])
    return held


def pick_kernel(block, first_place, num_slices, wanted_ref, *refs):
    slices, (out_ref, buffer, sems) = refs[:num_slices], refs[-3:]
    dests, slots, places = buffer.shape[:3]
    half = slices[0].shape[0]
    groups = sems.shape[0]
    each = dests // groups

    def one(step, carry):
        dest, slot = step // slots, step % slots
        start = pl.multiple_of(wanted_ref[dest, slot] * block, block)
        for index, ref in enumerate(slices):
            low = index % 2 * half
            buffer[dest, slot, index // 2, low : low + half, :] = ref[:, pl.ds(start, block)]
        return carry

    copies = []
    for group in range(groups):
        at = slice(group * each, group * each + each)
        lax.fori_loop(group * each * slots, (group + 1) * each * slots, one, 0, unroll=4)
        copies.append(
            pltpu.make_async_copy(
                buffer.at[at], out_ref.at[at, :, first_place : first_place + places], sems.at[group]
            )
        )
        copies[-1].start()
    for copy in copies:
        copy.wait()


def pick(wanted, slices, block, flops, places=None, before=None):
    askers, slots = wanted.shape
    count, rows = len(slices) // 2, 2 * slices[0].shape[0]
    places = before.shape[2] if before is not None else places or count
    first_place = places - count if before is not None else 0
    more = [] if before is None else [before]
    return pl.pallas_call(
        functools.partial(pick_kernel, block, first_place, len(slices)),
        out_shape=jax.ShapeDtypeStruct((askers, slots, places, rows, block), jnp.bfloat16),
        in_specs=[SMEM] + [VMEM] * len(slices) + [HBM] * len(more),
        out_specs=HBM,
        input_output_aliases={1 + len(slices): 0} if more else {},
        scratch_shapes=[pltpu.VMEM((askers, slots, count, rows, block), jnp.bfloat16), pltpu.SemaphoreType.DMA((4,))],
        compiler_params=params(58),
        cost_estimate=cost(flops, count * 2**21),
    )(wanted, *slices, *more)


def add_tiles(core, tgt_ref, count_ref, vals_ref, part, acc, ready):
    sections, slots, block, _ = vals_ref.shape
    places, rows = part.shape[2:4]
    acc[...] = jnp.zeros_like(acc)

    def one(section, slot):
        column = pl.multiple_of(tgt_ref[section, slot] * block, block)
        sources = [section * LANES + lane + core * (1 - 2 * (lane % 2)) for lane in range(LANES)]
        columns_in = jnp.concatenate([part[source, slot].reshape(places * rows, block) for source in sources])
        contrib = lax.dot_general(
            columns_in, vals_ref[section, slot], (((1,), (1,)), ((), ())), preferred_element_type=jnp.float32
        )
        for lane in range(LANES):
            for place in range(places):
                low, at = (place * LANES + lane) * rows, (lane * places + place) * rows
                acc[low : low + rows, pl.ds(column, block)] += contrib[at : at + rows]

    @pl.loop(0, sections)
    def _(section):
        ready(section)

        @pl.loop(0, jnp.minimum(count_ref[section], slots))
        def _(slot):
            one(section, slot)


def aggregate_kernel(core_ref, tgt_ref, count_ref, vals_ref, part, out_ref, acc):
    add_tiles(core_ref[0], tgt_ref, count_ref, vals_ref, part, acc, lambda section: None)
    out_ref[...] = acc[...].astype(out_ref.dtype)


def aggregate(core, targets, counts, values, part, num_rows):
    num_feats = LANES * part.shape[2] * part.shape[3]
    return pl.pallas_call(
        aggregate_kernel,
        out_shape=jax.ShapeDtypeStruct((num_feats, num_rows), jnp.bfloat16),
        in_specs=[SMEM] * 3 + [VMEM] * 2,
        out_specs=VMEM,
        scratch_shapes=[pltpu.VMEM((num_feats, num_rows), jnp.float32)],
        compiler_params=params(16),
        cost_estimate=cost(3 * 10**9, 8 * 2**20),
    )(core, targets, counts, values, part)


def layer_kernel(
    core_ref,
    tgt_ref,
    count_ref,
    vals_hbm,
    part_hbm,
    early_hbm,
    weight_hbm,
    cot_hbm,
    act_hbm,
    kept_ref,
    gone_ref,
    vals,
    part,
    weight,
    cot,
    act,
    acc,
    mixed,
    dpre,
    part_sems,
    sems,
    act_sems,
):
    early = early_hbm.shape[0]

    def section_copy(section):
        at = pl.ds(section * LANES, LANES)
        return pltpu.make_async_copy(part_hbm.at[at], part.at[at], part_sems.at[section])

    vals_copy = pltpu.make_async_copy(vals_hbm, vals, sems.at[0])
    early_copy = pltpu.make_async_copy(early_hbm, mixed.at[:early], sems.at[1])
    weight_copy = pltpu.make_async_copy(weight_hbm, weight, sems.at[2])
    cot_copy = pltpu.make_async_copy(cot_hbm, cot, sems.at[3])
    vals_copy.start()
    for section in range(part_sems.shape[0]):
        section_copy(section).start()
    for copy in (early_copy, weight_copy, cot_copy):
        copy.start()
    vals_copy.wait()
    add_tiles(core_ref[0], tgt_ref, count_ref, vals, part, acc, lambda section: section_copy(section).wait())
    mixed[early:] = acc[...].astype(mixed.dtype)
    for copy in (early_copy, weight_copy, cot_copy):
        copy.wait()

    step = act.shape[0] // act_sems.shape[0]
    act_copies = []
    for index in range(act_sems.shape[0]):
        at = slice(index * step, index * step + step)
        preact = lax.dot_general(
            mixed[:, at], weight[...], (((0,), (0,)), ((), ())), preferred_element_type=jnp.float32
        )
        sigmoid_val = jax.nn.sigmoid(preact)
        act[at] = (preact * sigmoid_val).astype(act.dtype)
        act_copies.append(pltpu.make_async_copy(act.at[at], act_hbm.at[at], act_sems.at[index]))
        act_copies[-1].start()
        slope = sigmoid_val * (1.0 + preact * (1.0 - sigmoid_val))
        dpre[at] = (cot[at].astype(jnp.float32) * slope).astype(dpre.dtype)
    pieces, _, _, rows, width = kept_ref.shape
    for low in range(0, mixed.shape[0], step):
        grad = jnp.dot(mixed[low : low + step], dpre[...], preferred_element_type=jnp.float32)
        for at in range(0, step, rows):
            lane = (low + at) // rows
            place, hi, core = lane // LANES, lane % LANES // 2, lane % 2
            for piece in range(pieces):
                value = grad[at : at + rows, piece * width : (piece + 1) * width]
                if core == 0:
                    kept_ref[piece, hi, place] = value
                else:
                    gone_ref[piece, hi, place] = value.astype(gone_ref.dtype)
    for copy in act_copies:
        copy.wait()


def layer(core, targets, counts, values, part, early, weight, cotangent):
    tgt_rows, width = cotangent.shape
    feats = weight.shape[0]
    cut = (8, 2, ZN, part.shape[3], width // 8)
    late = feats - early.shape[0]
    return pl.pallas_call(
        layer_kernel,
        out_shape=(
            jax.ShapeDtypeStruct((tgt_rows, width), jnp.bfloat16),
            jax.ShapeDtypeStruct(cut, jnp.float32),
            jax.ShapeDtypeStruct(cut, jnp.bfloat16),
        ),
        in_specs=[SMEM] * 3 + [HBM] * 5,
        out_specs=(HBM, VMEM, VMEM),
        scratch_shapes=[
            pltpu.VMEM(values.shape, values.dtype),
            pltpu.VMEM(part.shape, part.dtype),
            pltpu.VMEM(weight.shape, weight.dtype),
            pltpu.VMEM((tgt_rows, width), cotangent.dtype),
            pltpu.VMEM((tgt_rows, width), jnp.bfloat16),
            pltpu.VMEM((late, tgt_rows), jnp.float32),
            pltpu.VMEM((feats, tgt_rows), jnp.bfloat16),
            pltpu.VMEM((tgt_rows, width), jnp.bfloat16),
            pltpu.SemaphoreType.DMA((values.shape[0],)),
            pltpu.SemaphoreType.DMA((4,)),
            pltpu.SemaphoreType.DMA((4,)),
        ],
        compiler_params=params(56),
        cost_estimate=cost(6 * 10**9, 20 * 2**20),
    )(core, targets, counts, values, part, early, weight, cotangent)


def sum_plane_kernel(z_ref, came_ref, out_ref):
    for place, distance in enumerate(ORDER):
        total = came_ref[:, place].astype(jnp.float32).sum(0)
        out_ref[lax.rem(z_ref[0] + (ZN - distance), ZN)] = total


def sum_plane(came):
    return pl.pallas_call(
        sum_plane_kernel,
        out_shape=jax.ShapeDtypeStruct(came.shape[1:], jnp.float32),
        in_specs=[SMEM, VMEM],
        out_specs=VMEM,
        compiler_params=params(16),
    )(lax.axis_index("z").astype(jnp.int32)[None], came)


def sum_over_devices(kept, gone):
    came = lax.ppermute(gone, "core", SWAP)
    chip = (kept + came.astype(jnp.float32)).astype(jnp.bfloat16)
    chip = chip.reshape(16, *chip.shape[2:])
    plane = sum_plane(exchange(chip, CHIPS_XY))
    column = exchange(plane, "z").sum(0)
    whole = exchange(jnp.broadcast_to(column[None], (8, *column.shape)), REP)
    return whole.transpose(1, 0, 2).reshape(column.shape[0], -1)


def weight_lanes(own):
    other = lax.ppermute(own, ("ylo", "yhi"), [(0, 3), (1, 2), (2, 1), (3, 0)])
    first = lax.axis_index("yhi") == 0
    both = jnp.stack([jnp.where(first, own, other), jnp.where(first, other, own)])
    lanes = jnp.stack([both, lax.ppermute(both, "core", SWAP)], axis=1)
    return lanes.reshape(-1, own.shape[1])


def whole_weight(lanes):
    held = short_ring(lanes)
    return jnp.concatenate([held[distance] for distance in ORDER])


def per_device(features, tile_tgt, tile_src, tile_count, tile_vals, weight, cotangent):
    block_size = tile_vals.shape[-1]
    tgt_rows = cotangent.shape[0]
    targets, sources, counts, values = tile_tgt[0, 0], tile_src[0, 0], tile_count[0, 0], tile_vals[0, 0]
    core = lax.axis_index("core").astype(jnp.int32)[None]

    wanted = exchange(jnp.repeat(sources, LANES, axis=0)[:, None, :], PLANE)[:, 0]
    wanted, lanes = lax.optimization_barrier((wanted, weight_lanes(weight)))
    half = features.shape[1] // 2
    held = ring(features[0, :half], features[0, half:])
    first = pick(wanted, [piece for d in FIRST for piece in held[d]], block_size, PICK_FLOPS[0])
    early = aggregate(core, targets, counts, values, exchange(first, PLANE), tgt_rows)
    most = pick(wanted, [piece for d in SECOND[:-1] for piece in held[d]], block_size, PICK_FLOPS[1], len(SECOND))
    second = pick(wanted, held[SECOND[-1]], block_size, PICK_FLOPS[2], before=most)
    part = exchange(second, PLANE)
    weight_in = whole_weight(lanes)
    activations, kept, gone = layer(core, targets, counts, values, part, early, weight_in, cotangent)
    weight_grad = sum_over_devices(kept, gone) / math.sqrt(tgt_rows * 256)
    return (activations, weight_grad)


PICK_FLOPS = (25 * 10**9, 25 * 10**9, 1 * 10**9)


def solution(mesh):
    row = ("z", "yhi", "core")
    fine = Mesh(mesh.devices.reshape(2, 4, 8, 2, 2), ("ylo", "x", "z", "yhi", "core"))
    in_specs = (
        P(REP, row, None),
        P(REP, row, None, None),
        P(REP, row, None, None),
        P(REP, row, None),
        P(REP, row, None, None, None, None),
        P(row, None),
        P(REP + row, None),
    )
    out_specs = (P(REP + row, None), P(row, None))
    return jax.shard_map(per_device, mesh=fine, in_specs=in_specs, out_specs=out_specs, check_vma=False)
```

```python
import functools
import math

import jax
import jax.numpy as jnp
from jax import lax
from jax.experimental import pallas as pl
from jax.experimental.pallas import tpu as pltpu
from jax.sharding import Mesh, PartitionSpec as P

REP = ("ylo", "x")
PLANE = ("ylo", "x", "yhi", "core")
CHIPS_XY = ("ylo", "x", "yhi")
ZN = 8
PARTS = ((0, 1, -1), (2, -2, 3, -3), (4,))
ORDER = tuple(d for part in PARTS for d in part)
LANES = 4
LAYER_MIB = 56
VMEM = pl.BlockSpec(memory_space=pltpu.VMEM)
SMEM = pl.BlockSpec(memory_space=pltpu.SMEM)
HBM = pl.BlockSpec(memory_space=pltpu.HBM)
SWAP = [(0, 1), (1, 0)]


def params(mib):
    return pltpu.CompilerParams(vmem_limit_bytes=mib * 2**20)


def cost(flops, size):
    return pl.CostEstimate(flops=flops, bytes_accessed=size, transcendentals=0)


def shift_z(value, step):
    return lax.ppermute(value, "z", [(i, (i + step) % ZN) for i in range(ZN)])


def exchange(value, axes):
    return lax.all_to_all(value, axes, split_axis=0, concat_axis=0, tiled=True)


def ring(own):
    half = own.shape[0] // 2
    held = {0: own}
    for step in range(1, ZN // 2):
        held[step] = shift_z(held[step - 1], 1)
        held[-step] = shift_z(held[1 - step], -1)
    far = ZN // 2 - 1
    ends = [shift_z(held[far][:half], 1), shift_z(held[-far][half:], -1)]
    return {distance: [value] for distance, value in held.items()} | {ZN // 2: ends}


def pick_kernel(block, layout, wanted_ref, *refs):
    slices, (out_ref, buffer, sems) = refs[: len(layout)], refs[-3:]
    dests, slots = buffer.shape[:2]
    groups = sems.shape[0]
    each = dests // groups

    def one(step, carry):
        dest, slot = step // slots, step % slots
        start = pl.multiple_of(wanted_ref[dest, slot] * block, block)
        for ref, (place, low) in zip(slices, layout):
            buffer[dest, slot, place, low : low + ref.shape[0], :] = ref[:, pl.ds(start, block)]
        return carry

    copies = []
    for group in range(groups):
        at = slice(group * each, group * each + each)
        lax.fori_loop(group * each * slots, (group + 1) * each * slots, one, 0, unroll=4)
        copies.append(pltpu.make_async_copy(buffer.at[at], out_ref.at[at], sems.at[group]))
        copies[-1].start()
    for copy in copies:
        copy.wait()


def pick(wanted, slices, block, flops):
    askers, slots = wanted.shape
    count, rows = len(slices), sum(piece.shape[0] for piece in slices[0])
    layout = [(place, rows // len(pieces) * index) for place, pieces in enumerate(slices) for index in range(len(pieces))]
    refs = [piece for pieces in slices for piece in pieces]
    shape = (askers, slots, count, rows, block)
    return pl.pallas_call(
        functools.partial(pick_kernel, block, layout),
        out_shape=jax.ShapeDtypeStruct(shape, jnp.bfloat16),
        in_specs=[SMEM] + [VMEM] * len(refs),
        out_specs=HBM,
        scratch_shapes=[pltpu.VMEM(shape, jnp.bfloat16), pltpu.SemaphoreType.DMA((4,))],
        compiler_params=params(58),
        cost_estimate=cost(flops, count * 2**21),
    )(wanted, *refs)


def add_tiles(core, tgt_ref, count_ref, vals_ref, part, acc, ready):
    sections, slots, block, _ = vals_ref.shape
    places, rows = part.shape[2:4]
    acc[...] = jnp.zeros_like(acc)

    def one(section, slot):
        column = pl.multiple_of(tgt_ref[section, slot] * block, block)
        sources = [section * LANES + lane + core * (1 - 2 * (lane % 2)) for lane in range(LANES)]
        columns_in = jnp.concatenate([part[source, slot].reshape(places * rows, block) for source in sources])
        contrib = lax.dot_general(
            columns_in, vals_ref[section, slot], (((1,), (1,)), ((), ())), preferred_element_type=jnp.float32
        )
        for lane in range(LANES):
            for place in range(places):
                low, at = (place * LANES + lane) * rows, (lane * places + place) * rows
                acc[low : low + rows, pl.ds(column, block)] += contrib[at : at + rows]

    @pl.loop(0, sections)
    def _(section):
        ready(section)

        @pl.loop(0, jnp.minimum(count_ref[section], slots))
        def _(slot):
            one(section, slot)


def aggregate_kernel(core_ref, tgt_ref, count_ref, vals_ref, part, turned_ref, plain_ref, acc):
    add_tiles(core_ref[0], tgt_ref, count_ref, vals_ref, part, acc, lambda section: None)
    step = vals_ref.shape[-1]
    for low in range(0, acc.shape[1], step):
        at = slice(low, low + step)
        value = acc[:, at]
        turned_ref[:, at] = value.astype(turned_ref.dtype)
        plain_ref[at] = value.T.astype(plain_ref.dtype)


def aggregate(core, targets, counts, values, part, num_rows):
    num_feats = LANES * part.shape[2] * part.shape[3]
    return pl.pallas_call(
        aggregate_kernel,
        out_shape=(
            jax.ShapeDtypeStruct((num_feats, num_rows), jnp.bfloat16),
            jax.ShapeDtypeStruct((num_rows, num_feats), jnp.bfloat16),
        ),
        in_specs=[SMEM] * 3 + [VMEM] * 2,
        out_specs=(VMEM, VMEM),
        scratch_shapes=[pltpu.VMEM((num_feats, num_rows), jnp.float32)],
        compiler_params=params(20),
        cost_estimate=cost(3 * 10**9, 8 * 2**20),
    )(core, targets, counts, values, part)


def layer_kernel(num_early, core_ref, tgt_ref, count_ref, *refs):
    early, refs = refs[: 2 * num_early], refs[2 * num_early :]
    vals_hbm, part_hbm, weight_hbm, cot_hbm, act_hbm, kept_hbm, gone_hbm = refs[:7]
    vals, part, weight, cot, act, kept, gone, acc, turned, plain, dpre, part_sem, sems, early_sems, out_sems = refs[7:]
    part_copy = pltpu.make_async_copy(part_hbm, part, part_sem)
    vals_copy = pltpu.make_async_copy(vals_hbm, vals, sems.at[0])
    weight_copy = pltpu.make_async_copy(weight_hbm, weight, sems.at[1])
    cot_copy = pltpu.make_async_copy(cot_hbm, cot, sems.at[2])
    turned_copies, plain_copies = [], []
    low = 0
    for index in range(num_early):
        at = slice(low, low + early[2 * index].shape[0])
        low = at.stop
        turned_copies.append(pltpu.make_async_copy(early[2 * index], turned.at[at], early_sems.at[2 * index]))
        plain_copies.append(pltpu.make_async_copy(early[2 * index + 1], plain.at[:, at], early_sems.at[2 * index + 1]))
    for copy in (vals_copy, part_copy, *plain_copies, weight_copy, cot_copy, *turned_copies):
        copy.start()
    vals_copy.wait()
    part_copy.wait()
    add_tiles(core_ref[0], tgt_ref, count_ref, vals, part, acc, lambda section: None)
    width = vals.shape[-1]
    for first in range(0, acc.shape[1], width):
        at = slice(first, first + width)
        value = acc[:, at]
        turned[low:, at] = value.astype(turned.dtype)
        plain[at, low:] = value.T.astype(plain.dtype)
    for copy in (*plain_copies, weight_copy, cot_copy):
        copy.wait()

    blocks = out_sems.shape[1]
    step = act.shape[0] // blocks
    out_copies = []

    def send(source, target, sem):
        out_copies.append(pltpu.make_async_copy(source, target, sem))
        out_copies[-1].start()

    for index in range(blocks):
        at = slice(index * step, index * step + step)
        preact = jnp.dot(plain[at], weight[...], preferred_element_type=jnp.float32)
        sigmoid_val = jax.nn.sigmoid(preact)
        act[at] = (preact * sigmoid_val).astype(act.dtype)
        send(act.at[at], act_hbm.at[at], out_sems.at[0, index])
        slope = sigmoid_val * (1.0 + preact * (1.0 - sigmoid_val))
        dpre[at] = (cot[at].astype(jnp.float32) * slope).astype(dpre.dtype)
    for copy in turned_copies:
        copy.wait()
    pieces, _, _, rows, width = kept.shape
    step = turned.shape[0] // blocks
    for index in range(blocks):
        low = index * step
        grad = jnp.dot(turned[low : low + step], dpre[...], preferred_element_type=jnp.float32)
        for at in range(0, step, rows):
            lane = (low + at) // rows
            place, hi, core = lane // LANES, lane % LANES // 2, lane % 2
            for piece in range(pieces):
                value = grad[at : at + rows, piece * width : (piece + 1) * width]
                if core == 0:
                    kept[piece, hi, place] = value
                else:
                    gone[piece, hi, place] = value.astype(gone.dtype)
        done = slice(low // (LANES * rows), (low + step) // (LANES * rows))
        send(gone.at[:, :, done], gone_hbm.at[:, :, done], out_sems.at[1, index])
        send(kept.at[:, :, done], kept_hbm.at[:, :, done], out_sems.at[2, index])
    for copy in out_copies:
        copy.wait()


def layer(core, targets, counts, values, part, early, weight, cotangent):
    tgt_rows, width = cotangent.shape
    feats = weight.shape[0]
    cut = (8, 2, ZN, part.shape[3], width // 8)
    early = [value for pair in early for value in pair]
    late = feats - sum(value.shape[0] for value in early[::2])
    return pl.pallas_call(
        functools.partial(layer_kernel, len(early) // 2),
        out_shape=(
            jax.ShapeDtypeStruct((tgt_rows, width), jnp.bfloat16),
            jax.ShapeDtypeStruct(cut, jnp.float32),
            jax.ShapeDtypeStruct(cut, jnp.bfloat16),
        ),
        in_specs=[SMEM] * 3 + [HBM] * (len(early) + 4),
        out_specs=(HBM, HBM, HBM),
        scratch_shapes=[
            pltpu.VMEM(values.shape, values.dtype),
            pltpu.VMEM(part.shape, part.dtype),
            pltpu.VMEM(weight.shape, weight.dtype),
            pltpu.VMEM((tgt_rows, width), cotangent.dtype),
            pltpu.VMEM((tgt_rows, width), jnp.bfloat16),
            pltpu.VMEM(cut, jnp.float32),
            pltpu.VMEM(cut, jnp.bfloat16),
            pltpu.VMEM((late, tgt_rows), jnp.float32),
            pltpu.VMEM((feats, tgt_rows), jnp.bfloat16),
            pltpu.VMEM((tgt_rows, feats), jnp.bfloat16),
            pltpu.VMEM((tgt_rows, width), jnp.bfloat16),
            pltpu.SemaphoreType.DMA,
            pltpu.SemaphoreType.DMA((3,)),
            pltpu.SemaphoreType.DMA((len(early),)),
            pltpu.SemaphoreType.DMA((3, 4)),
        ],
        compiler_params=params(LAYER_MIB),
        cost_estimate=cost(6 * 10**9, 20 * 2**20),
    )(core, targets, counts, *early, values, part, weight, cotangent)


def sum_plane_kernel(z_ref, came_ref, out_ref):
    for place, distance in enumerate(ORDER):
        total = came_ref[:, place].astype(jnp.float32).sum(0)
        out_ref[lax.rem(z_ref[0] + (ZN - distance), ZN)] = total


def sum_plane(came):
    return pl.pallas_call(
        sum_plane_kernel,
        out_shape=jax.ShapeDtypeStruct(came.shape[1:], jnp.float32),
        in_specs=[SMEM, VMEM],
        out_specs=VMEM,
        compiler_params=params(16),
    )(lax.axis_index("z").astype(jnp.int32)[None], came)


def sum_over_devices(kept, gone):
    came = lax.ppermute(gone, "core", SWAP)
    chip = (kept + came.astype(jnp.float32)).astype(jnp.bfloat16)
    chip = chip.reshape(16, *chip.shape[2:])
    plane = sum_plane(exchange(chip, CHIPS_XY))
    column = exchange(plane, "z").sum(0)
    whole = exchange(jnp.broadcast_to(column[None], (8, *column.shape)), REP)
    return whole.transpose(1, 0, 2).reshape(column.shape[0], -1)


def weight_lanes(own):
    other = lax.ppermute(own, ("ylo", "yhi"), [(0, 3), (1, 2), (2, 1), (3, 0)])
    first = lax.axis_index("yhi") == 0
    return jnp.concatenate([jnp.where(first, own, other), jnp.where(first, other, own)])


def whole_weight(lanes):
    held = ring(lanes)
    mine = jnp.concatenate([piece for distance in ORDER for piece in held[distance]])
    other = lax.ppermute(mine, "core", SWAP)
    shape = (ZN * 2, lanes.shape[0] // 2, lanes.shape[1])
    return jnp.stack([mine.reshape(shape), other.reshape(shape)], axis=1).reshape(-1, lanes.shape[1])


def per_device(features, tile_tgt, tile_src, tile_count, tile_vals, weight, cotangent):
    block_size = tile_vals.shape[-1]
    tgt_rows = cotangent.shape[0]
    targets, sources, counts, values = tile_tgt[0, 0], tile_src[0, 0], tile_count[0, 0], tile_vals[0, 0]
    core = lax.axis_index("core").astype(jnp.int32)[None]

    wanted = exchange(jnp.repeat(sources, LANES, axis=0)[:, None, :], PLANE)[:, 0]
    wanted, lanes = lax.optimization_barrier((wanted, weight_lanes(weight)))
    held = ring(features[0])
    early = []
    for distances, flops in zip(PARTS, PICK_FLOPS):
        part = exchange(pick(wanted, [held[d] for d in distances], block_size, flops), PLANE)
        if distances != PARTS[-1]:
            early.append(aggregate(core, targets, counts, values, part, tgt_rows))
    weight_in = whole_weight(lanes)
    activations, kept, gone = layer(core, targets, counts, values, part, early, weight_in, cotangent)
    weight_grad = sum_over_devices(kept, gone) / math.sqrt(tgt_rows * 256)
    return (activations, weight_grad)


PICK_FLOPS = (20 * 10**9, 20 * 10**9, 1 * 10**9)


def solution(mesh):
    row = ("z", "yhi", "core")
    fine = Mesh(mesh.devices.reshape(2, 4, 8, 2, 2), ("ylo", "x", "z", "yhi", "core"))
    in_specs = (
        P(REP, row, None),
        P(REP, row, None, None),
        P(REP, row, None, None),
        P(REP, row, None),
        P(REP, row, None, None, None, None),
        P(row, None),
        P(REP + row, None),
    )
    out_specs = (P(REP + row, None), P(row, None))
    return jax.shard_map(per_device, mesh=fine, in_specs=in_specs, out_specs=out_specs, check_vma=False)
```

```python
import functools
import math

import jax
import jax.numpy as jnp
from jax import lax
from jax.experimental import pallas as pl
from jax.experimental.pallas import tpu as pltpu
from jax.sharding import Mesh, PartitionSpec as P

REP = ("ylo", "x")
PLANE = ("ylo", "x", "yhi", "core")
CHIPS_XY = ("ylo", "x", "yhi")
ZN = 8
PARTS = ((0, 1, -1), (2, -2, 3, -3), (4,))
ORDER = tuple(d for part in PARTS for d in part)
LANES = 4
LAYER_MIB = 56
VMEM = pl.BlockSpec(memory_space=pltpu.VMEM)
SMEM = pl.BlockSpec(memory_space=pltpu.SMEM)
HBM = pl.BlockSpec(memory_space=pltpu.HBM)
SWAP = [(0, 1), (1, 0)]


def params(mib):
    return pltpu.CompilerParams(vmem_limit_bytes=mib * 2**20)


def cost(flops, size):
    return pl.CostEstimate(flops=flops, bytes_accessed=size, transcendentals=0)


def shift_z(value, step):
    return lax.ppermute(value, "z", [(i, (i + step) % ZN) for i in range(ZN)])


def exchange(value, axes):
    return lax.all_to_all(value, axes, split_axis=0, concat_axis=0, tiled=True)


def ring(own):
    half = own.shape[0] // 2
    held = {0: own}
    for step in range(1, ZN // 2):
        held[step] = shift_z(held[step - 1], 1)
        held[-step] = shift_z(held[1 - step], -1)
    far = ZN // 2 - 1
    ends = [shift_z(held[far][:half], 1), shift_z(held[-far][half:], -1)]
    return {distance: [value] for distance, value in held.items()} | {ZN // 2: ends}


def pick_kernel(block, layout, wanted_ref, *refs):
    slices, (out_ref, buffer, sems) = refs[: len(layout)], refs[-3:]
    dests, slots = buffer.shape[:2]
    groups = sems.shape[0]
    each = dests // groups

    def one(step, carry):
        dest, slot = step // slots, step % slots
        start = pl.multiple_of(wanted_ref[dest, slot] * block, block)
        for ref, (place, low) in zip(slices, layout):
            buffer[dest, slot, place, low : low + ref.shape[0], :] = ref[:, pl.ds(start, block)]
        return carry

    copies = []
    for group in range(groups):
        at = slice(group * each, group * each + each)
        lax.fori_loop(group * each * slots, (group + 1) * each * slots, one, 0, unroll=4)
        copies.append(pltpu.make_async_copy(buffer.at[at], out_ref.at[at], sems.at[group]))
        copies[-1].start()
    for copy in copies:
        copy.wait()


def pick(wanted, slices, block, flops):
    askers, slots = wanted.shape
    count, rows = len(slices), sum(piece.shape[0] for piece in slices[0])
    layout = [(place, rows // len(pieces) * index) for place, pieces in enumerate(slices) for index in range(len(pieces))]
    refs = [piece for pieces in slices for piece in pieces]
    shape = (askers, slots, count, rows, block)
    return pl.pallas_call(
        functools.partial(pick_kernel, block, layout),
        out_shape=jax.ShapeDtypeStruct(shape, jnp.bfloat16),
        in_specs=[SMEM] + [VMEM] * len(refs),
        out_specs=HBM,
        scratch_shapes=[pltpu.VMEM(shape, jnp.bfloat16), pltpu.SemaphoreType.DMA((4,))],
        compiler_params=params(58),
        cost_estimate=cost(flops, count * 2**21),
    )(wanted, *refs)


def add_tiles(core, tgt_ref, count_ref, vals_ref, part, acc, ready):
    sections, slots, block, _ = vals_ref.shape
    places, rows = part.shape[2:4]
    acc[...] = jnp.zeros_like(acc)

    def one(section, slot):
        column = pl.multiple_of(tgt_ref[section, slot] * block, block)
        sources = [section * LANES + lane + core * (1 - 2 * (lane % 2)) for lane in range(LANES)]
        columns_in = jnp.concatenate([part[source, slot].reshape(places * rows, block) for source in sources])
        contrib = lax.dot_general(
            columns_in, vals_ref[section, slot], (((1,), (1,)), ((), ())), preferred_element_type=jnp.float32
        )
        for lane in range(LANES):
            for place in range(places):
                low, at = (place * LANES + lane) * rows, (lane * places + place) * rows
                acc[low : low + rows, pl.ds(column, block)] += contrib[at : at + rows]

    @pl.loop(0, sections)
    def _(section):
        ready(section)

        @pl.loop(0, jnp.minimum(count_ref[section], slots))
        def _(slot):
            one(section, slot)


def aggregate_kernel(core_ref, tgt_ref, count_ref, vals_ref, part, turned_ref, plain_ref, acc):
    add_tiles(core_ref[0], tgt_ref, count_ref, vals_ref, part, acc, lambda section: None)
    step = vals_ref.shape[-1]
    for low in range(0, acc.shape[1], step):
        at = slice(low, low + step)
        value = acc[:, at]
        turned_ref[:, at] = value.astype(turned_ref.dtype)
        plain_ref[at] = value.T.astype(plain_ref.dtype)


def aggregate(core, targets, counts, values, part, num_rows):
    num_feats = LANES * part.shape[2] * part.shape[3]
    return pl.pallas_call(
        aggregate_kernel,
        out_shape=(
            jax.ShapeDtypeStruct((num_feats, num_rows), jnp.bfloat16),
            jax.ShapeDtypeStruct((num_rows, num_feats), jnp.bfloat16),
        ),
        in_specs=[SMEM] * 3 + [VMEM] * 2,
        out_specs=(VMEM, VMEM),
        scratch_shapes=[pltpu.VMEM((num_feats, num_rows), jnp.float32)],
        compiler_params=params(20),
        cost_estimate=cost(3 * 10**9, 8 * 2**20),
    )(core, targets, counts, values, part)


def layer_kernel(num_early, core_ref, tgt_ref, count_ref, *refs):
    early, refs = refs[: 2 * num_early], refs[2 * num_early :]
    vals_hbm, part_hbm, weight_hbm, cot_hbm, act_hbm, kept_hbm, gone_hbm = refs[:7]
    vals, part, weight, cot, act, kept, gone, acc, turned, plain, dpre, sems, block_sems, out_sems = refs[7:]
    blocks = out_sems.shape[1]
    step = act.shape[0] // blocks
    vals_copy = pltpu.make_async_copy(vals_hbm, vals, sems.at[0])
    part_copy = pltpu.make_async_copy(part_hbm, part, sems.at[1])
    weight_copy = pltpu.make_async_copy(weight_hbm, weight, sems.at[2])
    block_copies = [[] for _ in range(blocks)]
    turned_copies = []
    for index, copies in enumerate(block_copies):
        at = slice(index * step, index * step + step)
        copies.append(pltpu.make_async_copy(cot_hbm.at[at], cot.at[at], block_sems.at[index, 0]))
        low = 0
        for number in range(num_early):
            columns = slice(low, low + early[2 * number].shape[0])
            low = columns.stop
            copies.append(
                pltpu.make_async_copy(early[2 * number + 1].at[at], plain.at[at, columns], block_sems.at[index, 1 + number])
            )
            if index == 0:
                turned_copies.append(pltpu.make_async_copy(early[2 * number], turned.at[columns], sems.at[3 + number]))
    for copy in (vals_copy, part_copy, weight_copy, *sum(block_copies, []), *turned_copies):
        copy.start()
    vals_copy.wait()
    part_copy.wait()
    add_tiles(core_ref[0], tgt_ref, count_ref, vals, part, acc, lambda section: None)
    width = vals.shape[-1]
    for first in range(0, acc.shape[1], width):
        at = slice(first, first + width)
        value = acc[:, at]
        turned[low:, at] = value.astype(turned.dtype)
        plain[at, low:] = value.T.astype(plain.dtype)
    weight_copy.wait()
    out_copies = []

    def send(source, target, sem):
        out_copies.append(pltpu.make_async_copy(source, target, sem))
        out_copies[-1].start()

    for index in range(blocks):
        at = slice(index * step, index * step + step)
        for copy in block_copies[index]:
            copy.wait()
        preact = jnp.dot(plain[at], weight[...], preferred_element_type=jnp.float32)
        sigmoid_val = jax.nn.sigmoid(preact)
        act[at] = (preact * sigmoid_val).astype(act.dtype)
        send(act.at[at], act_hbm.at[at], out_sems.at[0, index])
        slope = sigmoid_val * (1.0 + preact * (1.0 - sigmoid_val))
        dpre[at] = (cot[at].astype(jnp.float32) * slope).astype(dpre.dtype)
    for copy in turned_copies:
        copy.wait()
    pieces, _, _, rows, width = kept.shape
    step = turned.shape[0] // blocks
    for index in range(blocks):
        low = index * step
        grad = jnp.dot(turned[low : low + step], dpre[...], preferred_element_type=jnp.float32)
        for at in range(0, step, rows):
            lane = (low + at) // rows
            place, hi, core = lane // LANES, lane % LANES // 2, lane % 2
            for piece in range(pieces):
                value = grad[at : at + rows, piece * width : (piece + 1) * width]
                target = gone if core else kept
                target[piece, hi, place] = value.astype(target.dtype)
        done = slice(low // (LANES * rows), (low + step) // (LANES * rows))
        send(gone.at[:, :, done], gone_hbm.at[:, :, done], out_sems.at[1, index])
        send(kept.at[:, :, done], kept_hbm.at[:, :, done], out_sems.at[2, index])
    for copy in out_copies:
        copy.wait()


def layer(core, targets, counts, values, part, early, weight, cotangent):
    tgt_rows, width = cotangent.shape
    feats = weight.shape[0]
    cut = (8, 2, ZN, part.shape[3], width // 8)
    early = [value for pair in early for value in pair]
    late = feats - sum(value.shape[0] for value in early[::2])
    return pl.pallas_call(
        functools.partial(layer_kernel, len(early) // 2),
        out_shape=(
            jax.ShapeDtypeStruct((tgt_rows, width), jnp.bfloat16),
            jax.ShapeDtypeStruct(cut, jnp.bfloat16),
            jax.ShapeDtypeStruct(cut, jnp.bfloat16),
        ),
        in_specs=[SMEM] * 3 + [HBM] * (len(early) + 4),
        out_specs=(HBM, HBM, HBM),
        scratch_shapes=[
            pltpu.VMEM(values.shape, values.dtype),
            pltpu.VMEM(part.shape, part.dtype),
            pltpu.VMEM(weight.shape, weight.dtype),
            pltpu.VMEM((tgt_rows, width), cotangent.dtype),
            pltpu.VMEM((tgt_rows, width), jnp.bfloat16),
            pltpu.VMEM(cut, jnp.bfloat16),
            pltpu.VMEM(cut, jnp.bfloat16),
            pltpu.VMEM((late, tgt_rows), jnp.float32),
            pltpu.VMEM((feats, tgt_rows), jnp.bfloat16),
            pltpu.VMEM((tgt_rows, feats), jnp.bfloat16),
            pltpu.VMEM((tgt_rows, width), jnp.bfloat16),
            pltpu.SemaphoreType.DMA((3 + len(early) // 2,)),
            pltpu.SemaphoreType.DMA((4, 1 + len(early) // 2)),
            pltpu.SemaphoreType.DMA((3, 4)),
        ],
        compiler_params=params(LAYER_MIB),
        cost_estimate=cost(6 * 10**9, 20 * 2**20),
    )(core, targets, counts, *early, values, part, weight, cotangent)


def sum_plane_kernel(z_ref, came_ref, out_ref):
    for place, distance in enumerate(ORDER):
        total = came_ref[:, place].astype(jnp.float32).sum(0)
        out_ref[lax.rem(z_ref[0] + (ZN - distance), ZN)] = total


def sum_plane(came):
    return pl.pallas_call(
        sum_plane_kernel,
        out_shape=jax.ShapeDtypeStruct(came.shape[1:], jnp.float32),
        in_specs=[SMEM, VMEM],
        out_specs=VMEM,
        compiler_params=params(16),
    )(lax.axis_index("z").astype(jnp.int32)[None], came)


def sum_over_devices(kept, gone):
    came = lax.ppermute(gone, "core", SWAP)
    chip = (kept.astype(jnp.float32) + came.astype(jnp.float32)).astype(jnp.bfloat16)
    chip = chip.reshape(16, *chip.shape[2:])
    plane = sum_plane(exchange(chip, CHIPS_XY))
    column = exchange(plane, "z").sum(0)
    whole = exchange(jnp.broadcast_to(column[None], (8, *column.shape)), REP)
    return whole.transpose(1, 0, 2).reshape(column.shape[0], -1)


def weight_lanes(own):
    other = lax.ppermute(own, ("ylo", "yhi"), [(0, 3), (1, 2), (2, 1), (3, 0)])
    first = lax.axis_index("yhi") == 0
    return jnp.concatenate([jnp.where(first, own, other), jnp.where(first, other, own)])


def whole_weight(lanes):
    held = ring(lanes)
    mine = jnp.concatenate([piece for distance in ORDER for piece in held[distance]])
    other = lax.ppermute(mine, "core", SWAP)
    shape = (ZN * 2, lanes.shape[0] // 2, lanes.shape[1])
    return jnp.stack([mine.reshape(shape), other.reshape(shape)], axis=1).reshape(-1, lanes.shape[1])


def per_device(features, tile_tgt, tile_src, tile_count, tile_vals, weight, cotangent):
    block_size = tile_vals.shape[-1]
    tgt_rows = cotangent.shape[0]
    targets, sources, counts, values = tile_tgt[0, 0], tile_src[0, 0], tile_count[0, 0], tile_vals[0, 0]
    core = lax.axis_index("core").astype(jnp.int32)[None]

    wanted = exchange(jnp.repeat(sources, LANES, axis=0)[:, None, :], PLANE)[:, 0]
    wanted, lanes = lax.optimization_barrier((wanted, weight_lanes(weight)))
    held = ring(features[0])
    weight_in = whole_weight(lanes)
    early = []
    for distances, flops in zip(PARTS, PICK_FLOPS):
        if distances == PARTS[-1]:
            wanted, weight_in, early[0] = lax.optimization_barrier((wanted, weight_in, early[0]))
        part = exchange(pick(wanted, [held[d] for d in distances], block_size, flops), PLANE)
        if distances != PARTS[-1]:
            early.append(aggregate(core, targets, counts, values, part, tgt_rows))
    activations, kept, gone = layer(core, targets, counts, values, part, early, weight_in, cotangent)
    weight_grad = sum_over_devices(kept, gone) / math.sqrt(tgt_rows * 256)
    return (activations, weight_grad)


PICK_FLOPS = (20 * 10**9, 20 * 10**9, 1 * 10**9)


def solution(mesh):
    row = ("z", "yhi", "core")
    fine = Mesh(mesh.devices.reshape(2, 4, 8, 2, 2), ("ylo", "x", "z", "yhi", "core"))
    in_specs = (
        P(REP, row, None),
        P(REP, row, None, None),
        P(REP, row, None, None),
        P(REP, row, None),
        P(REP, row, None, None, None, None),
        P(row, None),
        P(REP + row, None),
    )
    out_specs = (P(REP + row, None), P(row, None))
    return jax.shard_map(per_device, mesh=fine, in_specs=in_specs, out_specs=out_specs, check_vma=False)
```

```python
import functools
import math

import jax
import jax.numpy as jnp
from jax import lax
from jax.experimental import pallas as pl
from jax.experimental.pallas import tpu as pltpu
from jax.sharding import Mesh, PartitionSpec as P

REP = ("ylo", "x")
PLANE = ("ylo", "x", "yhi", "core")
CHIPS_XY = ("ylo", "x", "yhi")
ZN = 8
PARTS = ((0, 1, -1), (2, -2, 3, -3), (4,))
ORDER = tuple(d for part in PARTS for d in part)
LANES = 4
EARLY_MIB = (20, 60)
LAYER_MIB = 50
VMEM = pl.BlockSpec(memory_space=pltpu.VMEM)
SMEM = pl.BlockSpec(memory_space=pltpu.SMEM)
HBM = pl.BlockSpec(memory_space=pltpu.HBM)
SWAP = [(0, 1), (1, 0)]


def params(mib):
    return pltpu.CompilerParams(vmem_limit_bytes=mib * 2**20)


def cost(flops, size):
    return pl.CostEstimate(flops=flops, bytes_accessed=size, transcendentals=0)


def shift_z(value, step):
    return lax.ppermute(value, "z", [(i, (i + step) % ZN) for i in range(ZN)])


def exchange(value, axes):
    return lax.all_to_all(value, axes, split_axis=0, concat_axis=0, tiled=True)


def ring(own):
    half = own.shape[0] // 2
    held = {0: own}
    for step in range(1, ZN // 2):
        held[step] = shift_z(held[step - 1], 1)
        held[-step] = shift_z(held[1 - step], -1)
    far = ZN // 2 - 1
    ends = [shift_z(held[far][:half], 1), shift_z(held[-far][half:], -1)]
    return {distance: [value] for distance, value in held.items()} | {ZN // 2: ends}


def pick_kernel(block, layout, wanted_ref, *refs):
    slices, (out_ref, buffer, sems) = refs[: len(layout)], refs[-3:]
    dests, slots = buffer.shape[:2]
    groups = sems.shape[0]
    each = dests // groups

    def one(step, carry):
        dest, slot = step // slots, step % slots
        start = pl.multiple_of(wanted_ref[dest, slot] * block, block)
        for ref, (place, low) in zip(slices, layout):
            buffer[dest, slot, place, low : low + ref.shape[0], :] = ref[:, pl.ds(start, block)]
        return carry

    copies = []
    for group in range(groups):
        at = slice(group * each, group * each + each)
        lax.fori_loop(group * each * slots, (group + 1) * each * slots, one, 0, unroll=4)
        copies.append(pltpu.make_async_copy(buffer.at[at], out_ref.at[at], sems.at[group]))
        copies[-1].start()
    for copy in copies:
        copy.wait()


def pick(wanted, slices, block, flops):
    askers, slots = wanted.shape
    count, rows = len(slices), sum(piece.shape[0] for piece in slices[0])
    layout = [(place, rows // len(pieces) * index) for place, pieces in enumerate(slices) for index in range(len(pieces))]
    refs = [piece for pieces in slices for piece in pieces]
    shape = (askers, slots, count, rows, block)
    return pl.pallas_call(
        functools.partial(pick_kernel, block, layout),
        out_shape=jax.ShapeDtypeStruct(shape, jnp.bfloat16),
        in_specs=[SMEM] + [VMEM] * len(refs),
        out_specs=HBM,
        scratch_shapes=[pltpu.VMEM(shape, jnp.bfloat16), pltpu.SemaphoreType.DMA((4,))],
        compiler_params=params(60),
        cost_estimate=cost(flops, count * 2**21),
    )(wanted, *refs)


def add_tiles(core, tgt_ref, count_ref, vals_ref, part, acc, live):
    sections, slots, block, _ = vals_ref.shape
    places, rows = part.shape[2:4]
    spare = acc.shape[1] - block
    acc[...] = jnp.zeros_like(acc)

    def enter(tile, found):
        live[found] = tile
        return found + (tile % slots < count_ref[tile // slots]).astype(jnp.int32)

    found = lax.fori_loop(0, sections * slots, enter, 0)
    each = 4

    @pl.loop(0, (found + each - 1) // each)
    def _(step):
        for index in range(each):
            at = step * each + index
            tile = jnp.where(at < found, live[jnp.minimum(at, sections * slots - 1)], 0)
            section, slot = tile // slots, tile % slots
            column = pl.multiple_of(jnp.where(at < found, tgt_ref[section, slot] * block, spare), block)
            sources = [section * LANES + lane + core * (1 - 2 * (lane % 2)) for lane in range(LANES)]
            columns_in = jnp.concatenate([part[source, slot].reshape(places * rows, block) for source in sources])
            contrib = lax.dot_general(
                columns_in, vals_ref[section, slot], (((1,), (1,)), ((), ())), preferred_element_type=jnp.float32
            )
            for lane in range(LANES):
                for place in range(places):
                    low, first = (place * LANES + lane) * rows, (lane * places + place) * rows
                    acc[low : low + rows, pl.ds(column, block)] += contrib[first : first + rows]


def aggregate_kernel(core_ref, tgt_ref, count_ref, vals_ref, part, turned_ref, plain_ref, acc, live):
    add_tiles(core_ref[0], tgt_ref, count_ref, vals_ref, part, acc, live)
    step = vals_ref.shape[-1]
    for low in range(0, turned_ref.shape[1], step):
        at = slice(low, low + step)
        value = acc[:, at]
        turned_ref[:, at] = value.astype(turned_ref.dtype)
        plain_ref[at] = value.T.astype(plain_ref.dtype)


def aggregate(core, targets, counts, values, part, num_rows, mib):
    num_feats = LANES * part.shape[2] * part.shape[3]
    return pl.pallas_call(
        aggregate_kernel,
        out_shape=(
            jax.ShapeDtypeStruct((num_feats, num_rows), jnp.bfloat16),
            jax.ShapeDtypeStruct((num_rows, num_feats), jnp.bfloat16),
        ),
        in_specs=[SMEM] * 3 + [VMEM] * 2,
        out_specs=(VMEM, VMEM),
        scratch_shapes=[
            pltpu.VMEM((num_feats, num_rows + values.shape[-1]), jnp.float32),
            pltpu.SMEM((values.shape[0] * values.shape[1],), jnp.int32),
        ],
        compiler_params=params(mib),
        cost_estimate=cost(3 * 10**9, 8 * 2**20),
    )(core, targets, counts, values, part)


def layer_kernel(num_early, core_ref, tgt_ref, count_ref, *refs):
    early, refs = refs[: 2 * num_early], refs[2 * num_early :]
    vals_hbm, part_hbm, weight_hbm, cot_hbm, act_hbm, kept_hbm, gone_hbm = refs[:7]
    vals, part, weight, cot, act, kept, gone, acc, live, turned, plain, dpre, sems, block_sems, out_sems = refs[7:]
    blocks = out_sems.shape[1]
    step = act.shape[0] // blocks
    vals_copy = pltpu.make_async_copy(vals_hbm, vals, sems.at[0])
    part_copy = pltpu.make_async_copy(part_hbm, part, sems.at[1])
    weight_copy = pltpu.make_async_copy(weight_hbm, weight, sems.at[2])
    block_copies = [[] for _ in range(blocks)]
    turned_copies = []
    for index, copies in enumerate(block_copies):
        at = slice(index * step, index * step + step)
        copies.append(pltpu.make_async_copy(cot_hbm.at[at], cot.at[at], block_sems.at[index, 0]))
        low = 0
        for number in range(num_early):
            columns = slice(low, low + early[2 * number].shape[0])
            low = columns.stop
            copies.append(
                pltpu.make_async_copy(early[2 * number + 1].at[at], plain.at[at, columns], block_sems.at[index, 1 + number])
            )
            if index == 0:
                turned_copies.append(pltpu.make_async_copy(early[2 * number], turned.at[columns], sems.at[3 + number]))
    for copy in (vals_copy, part_copy, weight_copy, *sum(block_copies, []), *turned_copies):
        copy.start()
    vals_copy.wait()
    part_copy.wait()
    add_tiles(core_ref[0], tgt_ref, count_ref, vals, part, acc, live)
    width = vals.shape[-1]
    for first in range(0, turned.shape[1], width):
        at = slice(first, first + width)
        value = acc[:, at]
        turned[low:, at] = value.astype(turned.dtype)
        plain[at, low:] = value.T.astype(plain.dtype)
    weight_copy.wait()
    out_copies = []

    def send(source, target, sem):
        out_copies.append(pltpu.make_async_copy(source, target, sem))
        out_copies[-1].start()

    for index in range(blocks):
        at = slice(index * step, index * step + step)
        for copy in block_copies[index]:
            copy.wait()
        preact = jnp.dot(plain[at], weight[...], preferred_element_type=jnp.float32)
        sigmoid_val = jax.nn.sigmoid(preact)
        act[at] = (preact * sigmoid_val).astype(act.dtype)
        send(act.at[at], act_hbm.at[at], out_sems.at[0, index])
        slope = sigmoid_val * (1.0 + preact * (1.0 - sigmoid_val))
        dpre[at] = (cot[at].astype(jnp.float32) * slope).astype(dpre.dtype)
    for copy in turned_copies:
        copy.wait()
    pieces, _, _, rows, width = kept.shape
    step = turned.shape[0] // blocks
    for index in range(blocks):
        low = index * step
        grad = jnp.dot(turned[low : low + step], dpre[...], preferred_element_type=jnp.float32)
        for at in range(0, step, rows):
            lane = (low + at) // rows
            place, hi, core = lane // LANES, lane % LANES // 2, lane % 2
            for piece in range(pieces):
                value = grad[at : at + rows, piece * width : (piece + 1) * width]
                target = gone if core else kept
                target[piece, hi, place] = value.astype(target.dtype)
        done = slice(low // (LANES * rows), (low + step) // (LANES * rows))
        send(gone.at[:, :, done], gone_hbm.at[:, :, done], out_sems.at[1, index])
        send(kept.at[:, :, done], kept_hbm.at[:, :, done], out_sems.at[2, index])
    for copy in out_copies:
        copy.wait()


def layer(core, targets, counts, values, part, early, weight, cotangent):
    tgt_rows, width = cotangent.shape
    feats = weight.shape[0]
    cut = (8, 2, ZN, part.shape[3], width // 8)
    early = [value for pair in early for value in pair]
    late = feats - sum(value.shape[0] for value in early[::2])
    return pl.pallas_call(
        functools.partial(layer_kernel, len(early) // 2),
        out_shape=(
            jax.ShapeDtypeStruct((tgt_rows, width), jnp.bfloat16),
            jax.ShapeDtypeStruct(cut, jnp.bfloat16),
            jax.ShapeDtypeStruct(cut, jnp.bfloat16),
        ),
        in_specs=[SMEM] * 3 + [HBM] * (len(early) + 4),
        out_specs=(HBM, HBM, HBM),
        scratch_shapes=[
            pltpu.VMEM(values.shape, values.dtype),
            pltpu.VMEM(part.shape, part.dtype),
            pltpu.VMEM(weight.shape, weight.dtype),
            pltpu.VMEM((tgt_rows, width), cotangent.dtype),
            pltpu.VMEM((tgt_rows, width), jnp.bfloat16),
            pltpu.VMEM(cut, jnp.bfloat16),
            pltpu.VMEM(cut, jnp.bfloat16),
            pltpu.VMEM((late, tgt_rows + values.shape[-1]), jnp.float32),
            pltpu.SMEM((values.shape[0] * values.shape[1],), jnp.int32),
            pltpu.VMEM((feats, tgt_rows), jnp.bfloat16),
            pltpu.VMEM((tgt_rows, feats), jnp.bfloat16),
            pltpu.VMEM((tgt_rows, width), jnp.bfloat16),
            pltpu.SemaphoreType.DMA((3 + len(early) // 2,)),
            pltpu.SemaphoreType.DMA((4, 1 + len(early) // 2)),
            pltpu.SemaphoreType.DMA((3, 4)),
        ],
        compiler_params=params(LAYER_MIB),
        cost_estimate=cost(6 * 10**9, 20 * 2**20),
    )(core, targets, counts, *early, values, part, weight, cotangent)


def sum_plane_kernel(z_ref, came_ref, out_ref):
    for place, distance in enumerate(ORDER):
        total = came_ref[:, place].astype(jnp.float32).sum(0)
        out_ref[lax.rem(z_ref[0] + (ZN - distance), ZN)] = total


def sum_plane(came):
    return pl.pallas_call(
        sum_plane_kernel,
        out_shape=jax.ShapeDtypeStruct(came.shape[1:], jnp.float32),
        in_specs=[SMEM, VMEM],
        out_specs=VMEM,
        compiler_params=params(16),
    )(lax.axis_index("z").astype(jnp.int32)[None], came)


def sum_over_devices(kept, gone):
    came = lax.ppermute(gone, "core", SWAP)
    chip = (kept.astype(jnp.float32) + came.astype(jnp.float32)).astype(jnp.bfloat16)
    chip = chip.reshape(16, *chip.shape[2:])
    plane = sum_plane(exchange(chip, CHIPS_XY))
    column = exchange(plane, "z").sum(0)
    whole = exchange(jnp.broadcast_to(column[None], (8, *column.shape)), REP)
    return whole.transpose(1, 0, 2).reshape(column.shape[0], -1)


def weight_lanes(own):
    other = lax.ppermute(own, ("ylo", "yhi"), [(0, 3), (1, 2), (2, 1), (3, 0)])
    first = lax.axis_index("yhi") == 0
    return jnp.concatenate([jnp.where(first, own, other), jnp.where(first, other, own)])


def whole_weight(lanes):
    held = ring(lanes)
    mine = jnp.concatenate([piece for distance in ORDER for piece in held[distance]])
    other = lax.ppermute(mine, "core", SWAP)
    shape = (ZN * 2, lanes.shape[0] // 2, lanes.shape[1])
    return jnp.stack([mine.reshape(shape), other.reshape(shape)], axis=1).reshape(-1, lanes.shape[1])


def per_device(features, tile_tgt, tile_src, tile_count, tile_vals, weight, cotangent):
    block_size = tile_vals.shape[-1]
    tgt_rows = cotangent.shape[0]
    targets, sources, counts, values = tile_tgt[0, 0], tile_src[0, 0], tile_count[0, 0], tile_vals[0, 0]
    core = lax.axis_index("core").astype(jnp.int32)[None]

    wanted = exchange(jnp.repeat(sources, LANES, axis=0)[:, None, :], PLANE)[:, 0]
    wanted, lanes = lax.optimization_barrier((wanted, weight_lanes(weight)))
    held = ring(features[0])
    weight_in = whole_weight(lanes)
    early = []
    for distances, flops in zip(PARTS, PICK_FLOPS):
        if distances == PARTS[-1]:
            wanted, weight_in, early[0] = lax.optimization_barrier((wanted, weight_in, early[0]))
        part = exchange(pick(wanted, [held[d] for d in distances], block_size, flops), PLANE)
        if distances != PARTS[-1]:
            early.append(aggregate(core, targets, counts, values, part, tgt_rows, EARLY_MIB[len(early)]))
    activations, kept, gone = layer(core, targets, counts, values, part, early, weight_in, cotangent)
    weight_grad = sum_over_devices(kept, gone) / math.sqrt(tgt_rows * 256)
    return (activations, weight_grad)


PICK_FLOPS = (20 * 10**9, 20 * 10**9, 1 * 10**9)


def solution(mesh):
    row = ("z", "yhi", "core")
    fine = Mesh(mesh.devices.reshape(2, 4, 8, 2, 2), ("ylo", "x", "z", "yhi", "core"))
    in_specs = (
        P(REP, row, None),
        P(REP, row, None, None),
        P(REP, row, None, None),
        P(REP, row, None),
        P(REP, row, None, None, None, None),
        P(row, None),
        P(REP + row, None),
    )
    out_specs = (P(REP + row, None), P(row, None))
    return jax.shard_map(per_device, mesh=fine, in_specs=in_specs, out_specs=out_specs, check_vma=False)
```

```python
import functools
import math

import jax
import jax.numpy as jnp
from jax import lax
from jax.experimental import pallas as pl
from jax.experimental.pallas import tpu as pltpu
from jax.sharding import Mesh, PartitionSpec as P

REP = ("ylo", "x")
PLANE = ("ylo", "x", "yhi", "core")
CHIPS_XY = ("ylo", "x", "yhi")
ZN = 8
PARTS = ((0, 1, -1), (2, -2, 3, -3), (4,))
ORDER = tuple(d for part in PARTS for d in part)
LANES = 4
EARLY_MIB = (20, 20)
LAYER_MIB = 50
VMEM = pl.BlockSpec(memory_space=pltpu.VMEM)
SMEM = pl.BlockSpec(memory_space=pltpu.SMEM)
HBM = pl.BlockSpec(memory_space=pltpu.HBM)
SWAP = [(0, 1), (1, 0)]


def params(mib):
    return pltpu.CompilerParams(vmem_limit_bytes=mib * 2**20)


def cost(flops, size):
    return pl.CostEstimate(flops=flops, bytes_accessed=size, transcendentals=0)


def shift_z(value, step):
    return lax.ppermute(value, "z", [(i, (i + step) % ZN) for i in range(ZN)])


def exchange(value, axes):
    return lax.all_to_all(value, axes, split_axis=0, concat_axis=0, tiled=True)


def ring(own):
    half = own.shape[0] // 2
    held = {0: own}
    for step in range(1, ZN // 2):
        held[step] = shift_z(held[step - 1], 1)
        held[-step] = shift_z(held[1 - step], -1)
    far = ZN // 2 - 1
    ends = [shift_z(held[far][:half], 1), shift_z(held[-far][half:], -1)]
    return {distance: [value] for distance, value in held.items()} | {ZN // 2: ends}


def pick_kernel(block, layout, wanted_ref, *refs):
    slices, (out_ref, buffer, sems) = refs[: len(layout)], refs[-3:]
    dests, slots = buffer.shape[:2]
    groups = sems.shape[0]
    each = dests // groups

    def one(step, carry):
        dest, slot = step // slots, step % slots
        start = pl.multiple_of(wanted_ref[dest, slot] * block, block)
        for ref, (place, low) in zip(slices, layout):
            buffer[dest, slot, place, low : low + ref.shape[0], :] = ref[:, pl.ds(start, block)]
        return carry

    copies = []
    for group in range(groups):
        at = slice(group * each, group * each + each)
        lax.fori_loop(group * each * slots, (group + 1) * each * slots, one, 0, unroll=4)
        copies.append(pltpu.make_async_copy(buffer.at[at], out_ref.at[at], sems.at[group]))
        copies[-1].start()
    for copy in copies:
        copy.wait()


def pick(wanted, slices, block, flops):
    askers, slots = wanted.shape
    count, rows = len(slices), sum(piece.shape[0] for piece in slices[0])
    layout = [(place, rows // len(pieces) * index) for place, pieces in enumerate(slices) for index in range(len(pieces))]
    refs = [piece for pieces in slices for piece in pieces]
    shape = (askers, slots, count, rows, block)
    return pl.pallas_call(
        functools.partial(pick_kernel, block, layout),
        out_shape=jax.ShapeDtypeStruct(shape, jnp.bfloat16),
        in_specs=[SMEM] + [VMEM] * len(refs),
        out_specs=HBM,
        scratch_shapes=[pltpu.VMEM(shape, jnp.bfloat16), pltpu.SemaphoreType.DMA((4,))],
        compiler_params=params(60),
        cost_estimate=cost(flops, count * 2**21),
    )(wanted, *refs)


def add_tiles(core, tgt_ref, count_ref, vals_ref, part, acc, live):
    sections, slots, block, _ = vals_ref.shape
    places, rows = part.shape[2:4]
    spare = acc.shape[1] - block
    acc[...] = jnp.zeros_like(acc)

    def enter(tile, found):
        live[found] = tile
        return found + (tile % slots < count_ref[tile // slots]).astype(jnp.int32)

    found = lax.fori_loop(0, sections * slots, enter, 0)
    each = 4

    @pl.loop(0, (found + each - 1) // each)
    def _(step):
        for index in range(each):
            at = step * each + index
            tile = jnp.where(at < found, live[jnp.minimum(at, sections * slots - 1)], 0)
            section, slot = tile // slots, tile % slots
            column = pl.multiple_of(jnp.where(at < found, tgt_ref[section, slot] * block, spare), block)
            sources = [section * LANES + lane + core * (1 - 2 * (lane % 2)) for lane in range(LANES)]
            columns_in = jnp.concatenate([part[source, slot].reshape(places * rows, block) for source in sources])
            contrib = lax.dot_general(
                columns_in, vals_ref[section, slot], (((1,), (1,)), ((), ())), preferred_element_type=jnp.float32
            )
            for lane in range(LANES):
                for place in range(places):
                    low, first = (place * LANES + lane) * rows, (lane * places + place) * rows
                    acc[low : low + rows, pl.ds(column, block)] += contrib[first : first + rows]


def aggregate_kernel(core_ref, tgt_ref, count_ref, vals_ref, part, turned_ref, plain_ref, acc, live):
    add_tiles(core_ref[0], tgt_ref, count_ref, vals_ref, part, acc, live)
    step = vals_ref.shape[-1]
    for low in range(0, turned_ref.shape[1], step):
        at = slice(low, low + step)
        value = acc[:, at]
        turned_ref[:, at] = value.astype(turned_ref.dtype)
        plain_ref[at] = value.T.astype(plain_ref.dtype)


def aggregate(core, targets, counts, values, part, num_rows, mib):
    num_feats = LANES * part.shape[2] * part.shape[3]
    return pl.pallas_call(
        aggregate_kernel,
        out_shape=(
            jax.ShapeDtypeStruct((num_feats, num_rows), jnp.bfloat16),
            jax.ShapeDtypeStruct((num_rows, num_feats), jnp.bfloat16),
        ),
        in_specs=[SMEM] * 3 + [VMEM] * 2,
        out_specs=(VMEM, VMEM),
        scratch_shapes=[
            pltpu.VMEM((num_feats, num_rows + values.shape[-1]), jnp.float32),
            pltpu.SMEM((values.shape[0] * values.shape[1],), jnp.int32),
        ],
        compiler_params=params(mib),
        cost_estimate=cost(3 * 10**9, 8 * 2**20),
    )(core, targets, counts, values, part)


def layer_kernel(num_early, core_ref, tgt_ref, count_ref, *refs):
    early, refs = refs[:num_early], refs[num_early:]
    vals_hbm, part_hbm, begun_hbm, weight_hbm, cot_hbm, act_hbm, kept_hbm, gone_hbm = refs[:8]
    vals, part, begun, weight, cot, act, kept, gone, acc, live, turned, plain, dpre, sems, block_sems, out_sems = refs[8:]
    blocks = out_sems.shape[1]
    step = act.shape[0] // blocks
    vals_copy = pltpu.make_async_copy(vals_hbm, vals, sems.at[0])
    part_copy = pltpu.make_async_copy(part_hbm, part, sems.at[1])
    weight_copy = pltpu.make_async_copy(weight_hbm, weight, sems.at[2])
    block_copies = [[] for _ in range(blocks)]
    turned_copies = []
    for index, copies in enumerate(block_copies):
        at = slice(index * step, index * step + step)
        copies.append(pltpu.make_async_copy(cot_hbm.at[at], cot.at[at], block_sems.at[index, 0]))
        copies.append(pltpu.make_async_copy(begun_hbm.at[at], begun.at[at], block_sems.at[index, 1]))
        low = 0
        for number in range(num_early):
            rows = slice(low, low + early[number].shape[0])
            low = rows.stop
            if index == 0:
                turned_copies.append(pltpu.make_async_copy(early[number], turned.at[rows], sems.at[3 + number]))
    for copy in (vals_copy, part_copy, weight_copy, *sum(block_copies, []), *turned_copies):
        copy.start()
    vals_copy.wait()
    part_copy.wait()
    add_tiles(core_ref[0], tgt_ref, count_ref, vals, part, acc, live)
    width = vals.shape[-1]
    for first in range(0, turned.shape[1], width):
        at = slice(first, first + width)
        value = acc[:, at]
        turned[low:, at] = value.astype(turned.dtype)
        plain[at] = value.T.astype(plain.dtype)
    weight_copy.wait()
    out_copies = []

    def send(source, target, sem):
        out_copies.append(pltpu.make_async_copy(source, target, sem))
        out_copies[-1].start()

    for index in range(blocks):
        at = slice(index * step, index * step + step)
        for copy in block_copies[index]:
            copy.wait()
        preact = begun[at] + jnp.dot(plain[at], weight[...], preferred_element_type=jnp.float32)
        sigmoid_val = jax.nn.sigmoid(preact)
        act[at] = (preact * sigmoid_val).astype(act.dtype)
        send(act.at[at], act_hbm.at[at], out_sems.at[0, index])
        slope = sigmoid_val * (1.0 + preact * (1.0 - sigmoid_val))
        dpre[at] = (cot[at].astype(jnp.float32) * slope).astype(dpre.dtype)
    for copy in turned_copies:
        copy.wait()
    pieces, _, _, rows, width = kept.shape
    step = turned.shape[0] // blocks
    for index in range(blocks):
        low = index * step
        grad = jnp.dot(turned[low : low + step], dpre[...], preferred_element_type=jnp.float32)
        for at in range(0, step, rows):
            lane = (low + at) // rows
            place, hi, core = lane // LANES, lane % LANES // 2, lane % 2
            for piece in range(pieces):
                value = grad[at : at + rows, piece * width : (piece + 1) * width]
                target = gone if core else kept
                target[piece, hi, place] = value.astype(target.dtype)
        done = slice(low // (LANES * rows), (low + step) // (LANES * rows))
        send(gone.at[:, :, done], gone_hbm.at[:, :, done], out_sems.at[1, index])
        send(kept.at[:, :, done], kept_hbm.at[:, :, done], out_sems.at[2, index])
    for copy in out_copies:
        copy.wait()


def layer(core, targets, counts, values, part, early, begun, weight, cotangent):
    tgt_rows, width = cotangent.shape
    late = weight.shape[0]
    feats = late + sum(value.shape[0] for value in early)
    cut = (8, 2, ZN, part.shape[3], width // 8)
    return pl.pallas_call(
        functools.partial(layer_kernel, len(early)),
        out_shape=(
            jax.ShapeDtypeStruct((tgt_rows, width), jnp.bfloat16),
            jax.ShapeDtypeStruct(cut, jnp.bfloat16),
            jax.ShapeDtypeStruct(cut, jnp.bfloat16),
        ),
        in_specs=[SMEM] * 3 + [HBM] * (len(early) + 5),
        out_specs=(HBM, HBM, HBM),
        scratch_shapes=[
            pltpu.VMEM(values.shape, values.dtype),
            pltpu.VMEM(part.shape, part.dtype),
            pltpu.VMEM(begun.shape, begun.dtype),
            pltpu.VMEM(weight.shape, weight.dtype),
            pltpu.VMEM((tgt_rows, width), cotangent.dtype),
            pltpu.VMEM((tgt_rows, width), jnp.bfloat16),
            pltpu.VMEM(cut, jnp.bfloat16),
            pltpu.VMEM(cut, jnp.bfloat16),
            pltpu.VMEM((late, tgt_rows + values.shape[-1]), jnp.float32),
            pltpu.SMEM((values.shape[0] * values.shape[1],), jnp.int32),
            pltpu.VMEM((feats, tgt_rows), jnp.bfloat16),
            pltpu.VMEM((tgt_rows, late), jnp.bfloat16),
            pltpu.VMEM((tgt_rows, width), jnp.bfloat16),
            pltpu.SemaphoreType.DMA((3 + len(early),)),
            pltpu.SemaphoreType.DMA((4, 2)),
            pltpu.SemaphoreType.DMA((3, 4)),
        ],
        compiler_params=params(LAYER_MIB),
        cost_estimate=cost(6 * 10**9, 20 * 2**20),
    )(core, targets, counts, *early, values, part, begun, weight, cotangent)


def sum_plane_kernel(z_ref, came_ref, out_ref):
    for place, distance in enumerate(ORDER):
        total = came_ref[:, place].astype(jnp.float32).sum(0)
        out_ref[lax.rem(z_ref[0] + (ZN - distance), ZN)] = total


def sum_plane(came):
    return pl.pallas_call(
        sum_plane_kernel,
        out_shape=jax.ShapeDtypeStruct(came.shape[1:], jnp.float32),
        in_specs=[SMEM, VMEM],
        out_specs=VMEM,
        compiler_params=params(16),
    )(lax.axis_index("z").astype(jnp.int32)[None], came)


def sum_over_devices(kept, gone):
    came = lax.ppermute(gone, "core", SWAP)
    chip = (kept.astype(jnp.float32) + came.astype(jnp.float32)).astype(jnp.bfloat16)
    chip = chip.reshape(16, *chip.shape[2:])
    plane = sum_plane(exchange(chip, CHIPS_XY))
    column = exchange(plane, "z").sum(0)
    whole = exchange(jnp.broadcast_to(column[None], (8, *column.shape)), REP)
    return whole.transpose(1, 0, 2).reshape(column.shape[0], -1)


def weight_lanes(own):
    other = lax.ppermute(own, ("ylo", "yhi"), [(0, 3), (1, 2), (2, 1), (3, 0)])
    first = lax.axis_index("yhi") == 0
    return jnp.concatenate([jnp.where(first, own, other), jnp.where(first, other, own)])


def whole_weight(lanes):
    held = ring(lanes)
    mine = jnp.concatenate([piece for distance in ORDER for piece in held[distance]])
    other = lax.ppermute(mine, "core", SWAP)
    shape = (ZN * 2, lanes.shape[0] // 2, lanes.shape[1])
    return jnp.stack([mine.reshape(shape), other.reshape(shape)], axis=1).reshape(-1, lanes.shape[1])


def per_device(features, tile_tgt, tile_src, tile_count, tile_vals, weight, cotangent):
    block_size = tile_vals.shape[-1]
    tgt_rows = cotangent.shape[0]
    targets, sources, counts, values = tile_tgt[0, 0], tile_src[0, 0], tile_count[0, 0], tile_vals[0, 0]
    core = lax.axis_index("core").astype(jnp.int32)[None]

    wanted = exchange(jnp.repeat(sources, LANES, axis=0)[:, None, :], PLANE)[:, 0]
    wanted, lanes = lax.optimization_barrier((wanted, weight_lanes(weight)))
    held = ring(features[0])
    weight_in = whole_weight(lanes)
    early = []
    for distances, flops in zip(PARTS, PICK_FLOPS):
        if distances == PARTS[-1]:
            wanted, weight_in, early[0] = lax.optimization_barrier((wanted, weight_in, early[0]))
        part = exchange(pick(wanted, [held[d] for d in distances], block_size, flops), PLANE)
        if distances != PARTS[-1]:
            early.append(aggregate(core, targets, counts, values, part, tgt_rows, EARLY_MIB[len(early)]))
    turned, plain = [pair[0] for pair in early], jnp.concatenate([pair[1] for pair in early], axis=1)
    split = plain.shape[1]
    begun = jnp.dot(plain, weight_in[:split], preferred_element_type=jnp.float32)
    activations, kept, gone = layer(core, targets, counts, values, part, turned, begun, weight_in[split:], cotangent)
    weight_grad = sum_over_devices(kept, gone) / math.sqrt(tgt_rows * 256)
    return (activations, weight_grad)


PICK_FLOPS = (20 * 10**9, 20 * 10**9, 1 * 10**9)


def solution(mesh):
    row = ("z", "yhi", "core")
    fine = Mesh(mesh.devices.reshape(2, 4, 8, 2, 2), ("ylo", "x", "z", "yhi", "core"))
    in_specs = (
        P(REP, row, None),
        P(REP, row, None, None),
        P(REP, row, None, None),
        P(REP, row, None),
        P(REP, row, None, None, None, None),
        P(row, None),
        P(REP + row, None),
    )
    out_specs = (P(REP + row, None), P(row, None))
    return jax.shard_map(per_device, mesh=fine, in_specs=in_specs, out_specs=out_specs, check_vma=False)
```

```python
import functools
import math

import jax
import jax.numpy as jnp
from jax import lax
from jax.experimental import pallas as pl
from jax.experimental.pallas import tpu as pltpu
from jax.sharding import Mesh, PartitionSpec as P

REP = ("ylo", "x")
PLANE = ("ylo", "x", "yhi", "core")
CHIPS_XY = ("ylo", "x", "yhi")
ZN = 8
PARTS = ((0, 1, -1), (2, -2, 3, -3), (4,))
ORDER = tuple(d for part in PARTS for d in part)
LANES = 4
EARLY_MIB = (20, 20)
LAYER_MIB = 50
VMEM = pl.BlockSpec(memory_space=pltpu.VMEM)
SMEM = pl.BlockSpec(memory_space=pltpu.SMEM)
HBM = pl.BlockSpec(memory_space=pltpu.HBM)
SWAP = [(0, 1), (1, 0)]


def params(mib):
    return pltpu.CompilerParams(vmem_limit_bytes=mib * 2**20)


def cost(flops, size):
    return pl.CostEstimate(flops=flops, bytes_accessed=size, transcendentals=0)


def shift_z(value, step):
    return lax.ppermute(value, "z", [(i, (i + step) % ZN) for i in range(ZN)])


def exchange(value, axes):
    return lax.all_to_all(value, axes, split_axis=0, concat_axis=0, tiled=True)


def ring(own):
    half = own.shape[0] // 2
    held = {0: own}
    for step in range(1, ZN // 2):
        held[step] = shift_z(held[step - 1], 1)
        held[-step] = shift_z(held[1 - step], -1)
    far = ZN // 2 - 1
    ends = [shift_z(held[far][:half], 1), shift_z(held[-far][half:], -1)]
    return {distance: [value] for distance, value in held.items()} | {ZN // 2: ends}


def pick_kernel(block, layout, wanted_ref, *refs):
    slices, (out_ref, buffer, sems) = refs[: len(layout)], refs[-3:]
    dests, slots = buffer.shape[:2]
    groups = sems.shape[0]
    each = dests // groups

    def one(step, carry):
        dest, slot = step // slots, step % slots
        start = pl.multiple_of(wanted_ref[dest, slot] * block, block)
        for ref, (place, low) in zip(slices, layout):
            buffer[dest, slot, place, low : low + ref.shape[0], :] = ref[:, pl.ds(start, block)]
        return carry

    copies = []
    for group in range(groups):
        at = slice(group * each, group * each + each)
        lax.fori_loop(group * each * slots, (group + 1) * each * slots, one, 0, unroll=4)
        copies.append(pltpu.make_async_copy(buffer.at[at], out_ref.at[at], sems.at[group]))
        copies[-1].start()
    for copy in copies:
        copy.wait()


def pick(wanted, slices, block, flops):
    askers, slots = wanted.shape
    count, rows = len(slices), sum(piece.shape[0] for piece in slices[0])
    layout = [(place, rows // len(pieces) * index) for place, pieces in enumerate(slices) for index in range(len(pieces))]
    refs = [piece for pieces in slices for piece in pieces]
    shape = (askers, slots, count, rows, block)
    return pl.pallas_call(
        functools.partial(pick_kernel, block, layout),
        out_shape=jax.ShapeDtypeStruct(shape, jnp.bfloat16),
        in_specs=[SMEM] + [VMEM] * len(refs),
        out_specs=HBM,
        scratch_shapes=[pltpu.VMEM(shape, jnp.bfloat16), pltpu.SemaphoreType.DMA((4,))],
        compiler_params=params(60),
        cost_estimate=cost(flops, count * 2**21),
    )(wanted, *refs)


def add_tiles(core, tgt_ref, count_ref, vals_ref, part, acc, live):
    sections, slots, block, _ = vals_ref.shape
    places, rows = part.shape[2:4]
    spare = acc.shape[1] - block
    acc[...] = jnp.zeros_like(acc)

    def enter(tile, found):
        live[found] = tile
        return found + (tile % slots < count_ref[tile // slots]).astype(jnp.int32)

    found = lax.fori_loop(0, sections * slots, enter, 0)
    each = 8

    @pl.loop(0, (found + each - 1) // each)
    def _(step):
        for index in range(each):
            at = step * each + index
            tile = jnp.where(at < found, live[jnp.minimum(at, sections * slots - 1)], 0)
            section, slot = tile // slots, tile % slots
            column = pl.multiple_of(jnp.where(at < found, tgt_ref[section, slot] * block, spare), block)
            sources = [section * LANES + lane + core * (1 - 2 * (lane % 2)) for lane in range(LANES)]
            columns_in = jnp.concatenate([part[source, slot].reshape(places * rows, block) for source in sources])
            contrib = lax.dot_general(
                columns_in, vals_ref[section, slot], (((1,), (1,)), ((), ())), preferred_element_type=jnp.float32
            )
            for lane in range(LANES):
                for place in range(places):
                    low, first = (place * LANES + lane) * rows, (lane * places + place) * rows
                    acc[low : low + rows, pl.ds(column, block)] += contrib[first : first + rows]


def aggregate_kernel(core_ref, tgt_ref, count_ref, vals_ref, part, turned_ref, plain_ref, acc, live):
    add_tiles(core_ref[0], tgt_ref, count_ref, vals_ref, part, acc, live)
    step = vals_ref.shape[-1]
    for low in range(0, turned_ref.shape[1], step):
        at = slice(low, low + step)
        value = acc[:, at]
        turned_ref[:, at] = value.astype(turned_ref.dtype)
        plain_ref[at] = value.T.astype(plain_ref.dtype)


def aggregate(core, targets, counts, values, part, num_rows, mib):
    num_feats = LANES * part.shape[2] * part.shape[3]
    return pl.pallas_call(
        aggregate_kernel,
        out_shape=(
            jax.ShapeDtypeStruct((num_feats, num_rows), jnp.bfloat16),
            jax.ShapeDtypeStruct((num_rows, num_feats), jnp.bfloat16),
        ),
        in_specs=[SMEM] * 3 + [VMEM] * 2,
        out_specs=(VMEM, VMEM),
        scratch_shapes=[
            pltpu.VMEM((num_feats, num_rows + values.shape[-1]), jnp.float32),
            pltpu.SMEM((values.shape[0] * values.shape[1],), jnp.int32),
        ],
        compiler_params=params(mib),
        cost_estimate=cost(3 * 10**9, 8 * 2**20),
    )(core, targets, counts, values, part)


def layer_kernel(num_early, core_ref, tgt_ref, count_ref, *refs):
    early, refs = refs[:num_early], refs[num_early:]
    vals_hbm, part_hbm, begun_hbm, weight_hbm, cot_hbm, act_hbm, kept_hbm, gone_hbm = refs[:8]
    vals, part, begun, weight, cot, act, kept, gone, acc, live, turned, plain, dpre, sems, block_sems, out_sems = refs[8:]
    blocks = out_sems.shape[1]
    step = act.shape[0] // blocks
    vals_copy = pltpu.make_async_copy(vals_hbm, vals, sems.at[0])
    part_copy = pltpu.make_async_copy(part_hbm, part, sems.at[1])
    weight_copy = pltpu.make_async_copy(weight_hbm, weight, sems.at[2])
    block_copies = [[] for _ in range(blocks)]
    turned_copies = []
    for index, copies in enumerate(block_copies):
        at = slice(index * step, index * step + step)
        copies.append(pltpu.make_async_copy(cot_hbm.at[at], cot.at[at], block_sems.at[index, 0]))
        copies.append(pltpu.make_async_copy(begun_hbm.at[at], begun.at[at], block_sems.at[index, 1]))
        low = 0
        for number in range(num_early):
            rows = slice(low, low + early[number].shape[0])
            low = rows.stop
            if index == 0:
                turned_copies.append(pltpu.make_async_copy(early[number], turned.at[rows], sems.at[3 + number]))
    for copy in (vals_copy, part_copy, weight_copy, *sum(block_copies, []), *turned_copies):
        copy.start()
    vals_copy.wait()
    part_copy.wait()
    add_tiles(core_ref[0], tgt_ref, count_ref, vals, part, acc, live)
    width = vals.shape[-1]
    for first in range(0, turned.shape[1], width):
        at = slice(first, first + width)
        value = acc[:, at]
        turned[low:, at] = value.astype(turned.dtype)
        plain[at] = value.T.astype(plain.dtype)
    weight_copy.wait()
    out_copies = []

    def send(source, target, sem):
        out_copies.append(pltpu.make_async_copy(source, target, sem))
        out_copies[-1].start()

    for index in range(blocks):
        at = slice(index * step, index * step + step)
        for copy in block_copies[index]:
            copy.wait()
        preact = begun[at] + jnp.dot(plain[at], weight[...], preferred_element_type=jnp.float32)
        sigmoid_val = 0.5 * jnp.tanh(0.5 * preact) + 0.5
        act[at] = (preact * sigmoid_val).astype(act.dtype)
        send(act.at[at], act_hbm.at[at], out_sems.at[0, index])
        slope = sigmoid_val * (1.0 + preact * (1.0 - sigmoid_val))
        dpre[at] = (cot[at].astype(jnp.float32) * slope).astype(dpre.dtype)
    for copy in turned_copies:
        copy.wait()
    pieces, _, _, rows, width = kept.shape
    step = turned.shape[0] // blocks
    for index in range(blocks):
        low = index * step
        grad = jnp.dot(turned[low : low + step], dpre[...], preferred_element_type=jnp.float32)
        for at in range(0, step, rows):
            lane = (low + at) // rows
            place, hi, core = lane // LANES, lane % LANES // 2, lane % 2
            for piece in range(pieces):
                value = grad[at : at + rows, piece * width : (piece + 1) * width]
                target = gone if core else kept
                target[piece, hi, place] = value.astype(target.dtype)
        done = slice(low // (LANES * rows), (low + step) // (LANES * rows))
        send(gone.at[:, :, done], gone_hbm.at[:, :, done], out_sems.at[1, index])
        send(kept.at[:, :, done], kept_hbm.at[:, :, done], out_sems.at[2, index])
    for copy in out_copies:
        copy.wait()


def layer(core, targets, counts, values, part, early, begun, weight, cotangent):
    tgt_rows, width = cotangent.shape
    late = weight.shape[0]
    feats = late + sum(value.shape[0] for value in early)
    cut = (8, 2, ZN, part.shape[3], width // 8)
    return pl.pallas_call(
        functools.partial(layer_kernel, len(early)),
        out_shape=(
            jax.ShapeDtypeStruct((tgt_rows, width), jnp.bfloat16),
            jax.ShapeDtypeStruct(cut, jnp.bfloat16),
            jax.ShapeDtypeStruct(cut, jnp.bfloat16),
        ),
        in_specs=[SMEM] * 3 + [HBM] * (len(early) + 5),
        out_specs=(HBM, HBM, HBM),
        scratch_shapes=[
            pltpu.VMEM(values.shape, values.dtype),
            pltpu.VMEM(part.shape, part.dtype),
            pltpu.VMEM(begun.shape, begun.dtype),
            pltpu.VMEM(weight.shape, weight.dtype),
            pltpu.VMEM((tgt_rows, width), cotangent.dtype),
            pltpu.VMEM((tgt_rows, width), jnp.bfloat16),
            pltpu.VMEM(cut, jnp.bfloat16),
            pltpu.VMEM(cut, jnp.bfloat16),
            pltpu.VMEM((late, tgt_rows + values.shape[-1]), jnp.float32),
            pltpu.SMEM((values.shape[0] * values.shape[1],), jnp.int32),
            pltpu.VMEM((feats, tgt_rows), jnp.bfloat16),
            pltpu.VMEM((tgt_rows, late), jnp.bfloat16),
            pltpu.VMEM((tgt_rows, width), jnp.bfloat16),
            pltpu.SemaphoreType.DMA((3 + len(early),)),
            pltpu.SemaphoreType.DMA((4, 2)),
            pltpu.SemaphoreType.DMA((3, 4)),
        ],
        compiler_params=params(LAYER_MIB),
        cost_estimate=cost(6 * 10**9, 20 * 2**20),
    )(core, targets, counts, *early, values, part, begun, weight, cotangent)


def sum_plane_kernel(z_ref, came_ref, out_ref):
    for place, distance in enumerate(ORDER):
        total = came_ref[:, place].astype(jnp.float32).sum(0)
        out_ref[lax.rem(z_ref[0] + (ZN - distance), ZN)] = total


def sum_plane(came):
    return pl.pallas_call(
        sum_plane_kernel,
        out_shape=jax.ShapeDtypeStruct(came.shape[1:], jnp.float32),
        in_specs=[SMEM, VMEM],
        out_specs=VMEM,
        compiler_params=params(16),
    )(lax.axis_index("z").astype(jnp.int32)[None], came)


def sum_over_devices(kept, gone):
    came = lax.ppermute(gone, "core", SWAP)
    chip = (kept.astype(jnp.float32) + came.astype(jnp.float32)).astype(jnp.bfloat16)
    chip = chip.reshape(16, *chip.shape[2:])
    plane = sum_plane(exchange(chip, CHIPS_XY))
    column = exchange(plane, "z").sum(0)
    whole = exchange(jnp.broadcast_to(column[None], (8, *column.shape)), REP)
    return whole.transpose(1, 0, 2).reshape(column.shape[0], -1)


def weight_lanes(own):
    other = lax.ppermute(own, ("ylo", "yhi"), [(0, 3), (1, 2), (2, 1), (3, 0)])
    first = lax.axis_index("yhi") == 0
    return jnp.concatenate([jnp.where(first, own, other), jnp.where(first, other, own)])


def whole_weight(lanes):
    held = ring(lanes)
    mine = jnp.concatenate([piece for distance in ORDER for piece in held[distance]])
    other = lax.ppermute(mine, "core", SWAP)
    shape = (ZN * 2, lanes.shape[0] // 2, lanes.shape[1])
    return jnp.stack([mine.reshape(shape), other.reshape(shape)], axis=1).reshape(-1, lanes.shape[1])


def per_device(features, tile_tgt, tile_src, tile_count, tile_vals, weight, cotangent):
    block_size = tile_vals.shape[-1]
    tgt_rows = cotangent.shape[0]
    targets, sources, counts, values = tile_tgt[0, 0], tile_src[0, 0], tile_count[0, 0], tile_vals[0, 0]
    core = lax.axis_index("core").astype(jnp.int32)[None]

    wanted = exchange(jnp.repeat(sources, LANES, axis=0)[:, None, :], PLANE)[:, 0]
    wanted, lanes = lax.optimization_barrier((wanted, weight_lanes(weight)))
    held = ring(features[0])
    weight_in = whole_weight(lanes)
    early = []
    for distances, flops in zip(PARTS, PICK_FLOPS):
        if distances == PARTS[-1]:
            wanted, weight_in, early[0] = lax.optimization_barrier((wanted, weight_in, early[0]))
        part = exchange(pick(wanted, [held[d] for d in distances], block_size, flops), PLANE)
        if distances != PARTS[-1]:
            early.append(aggregate(core, targets, counts, values, part, tgt_rows, EARLY_MIB[len(early)]))
    turned, plain = [pair[0] for pair in early], jnp.concatenate([pair[1] for pair in early], axis=1)
    split = plain.shape[1]
    begun = jnp.dot(plain, weight_in[:split], preferred_element_type=jnp.float32)
    activations, kept, gone = layer(core, targets, counts, values, part, turned, begun, weight_in[split:], cotangent)
    weight_grad = sum_over_devices(kept, gone) / math.sqrt(tgt_rows * 256)
    return (activations, weight_grad)


PICK_FLOPS = (20 * 10**9, 20 * 10**9, 1 * 10**9)


def solution(mesh):
    row = ("z", "yhi", "core")
    fine = Mesh(mesh.devices.reshape(2, 4, 8, 2, 2), ("ylo", "x", "z", "yhi", "core"))
    in_specs = (
        P(REP, row, None),
        P(REP, row, None, None),
        P(REP, row, None, None),
        P(REP, row, None),
        P(REP, row, None, None, None, None),
        P(row, None),
        P(REP + row, None),
    )
    out_specs = (P(REP + row, None), P(row, None))
    return jax.shard_map(per_device, mesh=fine, in_specs=in_specs, out_specs=out_specs, check_vma=False)
```
